32 devices in a mesh: flow: 8 (over y, x, core), chem: 4 (over z).
Axes of the slice: x: 2, y: 2, z: 4, core: 2. Of those that a mesh axis runs over, the one named last changes fastest.
Arguments:
- component_levels: float32 [512, 111, 512], P('flow', None, 'chem'), may hold values from 0.1 to 2
- thermal_field: float32 [512, 512], P('flow', 'chem'), may hold values from 0.5 to 2.7
- reciprocal_pair_diffusivity: float32 [111, 111], replicated, may hold values from 0.005 to 0.02
- log_arrhenius_factor: float32 [784], replicated, may hold values from -1 to 6
- kinetic_exponents: float32 [784, 111], replicated, may hold values from 0 to 0.05
- arrhenius_energies: float32 [784], replicated, may hold values from 0.5 to 4
- molar_change_matrix: float32 [111, 784], replicated, may hold values from -0.21875 to 0.21875
- cooling_by_component: float32 [111], replicated, may hold values from -1 to 1
- burning_flags: int32 [512, 4], P('flow', 'chem'), may hold values from 0 to 1, as said below
Outputs:
- advanced_components: float32 [512, 111, 512], P('flow', None, 'chem')
- advanced_thermal: float32 [512, 512], P('flow', 'chem')
The draws below stay inside these ranges and needn't reach their ends.
Inputs may be any that keep to these rules, and one draw needn't show every extreme that they name: `burning_flags`: each device's 64 rows hold at most 24 reacting blocks, and at least one device of every chem index holds exactly 24; the devices of one chem index hold exactly 64 reacting blocks together.
All inputs are finite; a program needn't handle non-finite values.
Results may differ from the reference program's by a relative error of at most 0.000058.
Values sent between devices are 32-bit elements; how exact they have to be, the bound alone decides.
A program may use at most 192 MiB of HBM per device.

```python
import math
from functools import partial
import jax
import jax.numpy as jnp
from jax import lax

COMPONENTS = 111
R = 784
PATCH_POINTS = 128
CX = 64
AVG = 8
MOST = 24
LEADING_POINTS = 512
TRAILING_POINTS = 512
N_FLOW = 8
N_CHEM = 4


def draw_thermal_field(key, part):
    noise_key = jax.random.fold_in(key, 11)
    ramp = (jnp.arange(LEADING_POINTS, dtype=jnp.float32) / max(LEADING_POINTS - 1, 1))[:, None]
    rough = jax.random.uniform(noise_key, (LEADING_POINTS, TRAILING_POINTS), jnp.float32, -0.2, 0.2)
    return 0.7 + 1.4 * ramp + rough


def column_counts(key):
    moves = 4 * N_FLOW
    keys = jax.random.split(key, 4)
    givers = jax.random.randint(keys[0], (moves,), 0, N_FLOW)
    takers = jax.random.randint(keys[1], (moves,), 0, N_FLOW)
    amounts = jax.random.randint(keys[2], (moves,), 0, MOST + 1)
    leader = jax.random.randint(keys[3], (), 0, N_FLOW)

    def shuffle(index, counts):
        giver = givers[index]
        taker = takers[index]
        amount = jnp.minimum(amounts[index], jnp.minimum(counts[giver], MOST - counts[taker]))
        amount = jnp.where(giver == taker, 0, amount)
        return counts.at[giver].add(-amount).at[taker].add(amount)
    counts = lax.fori_loop(0, moves, shuffle, jnp.full((N_FLOW,), AVG, jnp.int32))

    def gather_up(index, counts):
        amount = jnp.minimum(counts[index], MOST - counts[leader])
        amount = jnp.where(index == leader, 0, amount)
        return counts.at[index].add(-amount).at[leader].add(amount)
    return lax.fori_loop(0, N_FLOW, gather_up, counts)


def draw_burning_flags(key, part):

    def column(column_key):
        count_key, place_key = jax.random.split(column_key)
        counts = column_counts(count_key)
        orders = jax.vmap(lambda inner: jax.random.permutation(inner, CX))(jax.random.split(place_key, N_FLOW))
        return (orders < counts[:, None]).astype(jnp.int32).reshape(LEADING_POINTS)
    columns = jax.vmap(column)(jax.random.split(jax.random.fold_in(key, 29), N_CHEM))
    return columns.T


def block_scale(stream_key, dims, cuts, low, largest):
    def one(axis_at, parts):
        heights = jax.random.uniform(jax.random.fold_in(jax.random.fold_in(stream_key, 6), axis_at), (parts,), jnp.float32, low / len(cuts), largest / len(cuts))
        return jnp.repeat(jnp.exp(heights), dims[axis_at] // parts).reshape((-1,) + (1,) * (len(dims) - axis_at - 1))

    gain = one(*cuts[0])
    for cut in cuts[1:]:
        gain = gain * one(*cut)
    return gain


def gaussian(own_key, extent, spread, limit, held_as=jnp.bfloat16):
    return jnp.clip(spread * jax.random.normal(own_key, extent, jnp.float32), -limit, limit).astype(held_as)


def setup_inputs(seed: int = 0) -> dict:
    seeds = jax.random.split(jax.random.key(seed), 10)
    component_levels = jnp.clip(jnp.exp(math.log(2.0) - 2.9957323 * jax.random.uniform(seeds[0], (LEADING_POINTS, COMPONENTS, TRAILING_POINTS), jnp.float32) ** block_scale(seeds[0], (LEADING_POINTS, COMPONENTS, TRAILING_POINTS), ((0, 8), (2, 4)), -0.2, 0.2)), 0.1, 2.0)
    thermal_field = draw_thermal_field(jax.random.fold_in(seeds[9], 71), 0)
    reciprocal_pair_diffusivity = jnp.clip(jnp.exp(jax.random.uniform(seeds[2], (COMPONENTS, COMPONENTS), jnp.float32, math.log(0.005), math.log(0.02))), 0.005, 0.02)
    log_arrhenius_factor = jnp.clip(jax.random.uniform(seeds[3], (R,), jnp.float32, -1.0, 6.0), -1.0, 6.0)
    kinetic_exponents = jnp.clip(jax.random.uniform(seeds[4], (R, COMPONENTS), jnp.float32, 0.0, 0.05), 0.0, 0.05)
    arrhenius_energies = jnp.clip(jax.random.uniform(seeds[5], (R,), jnp.float32, 0.5, 4.0), 0.5, 4.0)
    molar_change_matrix = gaussian(seeds[6], (COMPONENTS, R), R ** -0.5, 0.21875, jnp.float32)
    cooling_by_component = gaussian(seeds[7], (COMPONENTS,), 0.2, 1.0, jnp.float32)
    burning_flags = draw_burning_flags(jax.random.fold_in(seeds[9], 71), 0)
    return {"component_levels": component_levels, "thermal_field": thermal_field, "reciprocal_pair_diffusivity": reciprocal_pair_diffusivity, "log_arrhenius_factor": log_arrhenius_factor, "kinetic_exponents": kinetic_exponents, "arrhenius_energies": arrhenius_energies, "molar_change_matrix": molar_change_matrix, "cooling_by_component": cooling_by_component, "burning_flags": burning_flags}


maximal_load = lax.Precision.HIGHEST
courant = 0.2
chem_step = 0.05
log_offset = 0.001
rate_ceiling = 2.0

def blend_mean(component_levels, thermal_field, reciprocal_pair_diffusivity):
    denominator = jnp.einsum('kj,xjy->xky', reciprocal_pair_diffusivity, component_levels, precision=maximal_load)
    scaled_thermal_field = thermal_field * jnp.sqrt(thermal_field)
    return scaled_thermal_field[:, None, :] / denominator

def diffuse(padded_species, padded_diffusivity, time_step):
    row_count = padded_species.shape[0] - 2
    col_count = padded_species.shape[2] - 2
    center = padded_species[1:-1, :, 1:-1]
    center_diff = padded_diffusivity[1:-1, :, 1:-1]
    flux_sum = jnp.zeros_like(center)
    for row_shift, col_shift in ((0, 1), (2, 1), (1, 0), (1, 2)):
        neighbour = padded_species[row_shift:row_shift + row_count, :, col_shift:col_shift + col_count]
        neighbour_diff = padded_diffusivity[row_shift:row_shift + row_count, :, col_shift:col_shift + col_count]
        flux_sum = flux_sum + 0.5 * (center_diff + neighbour_diff) * (neighbour - center)
    return center + time_step * flux_sum

def production(state, inverse_theta, log_arrhenius_factor, kinetic_exponents, arrhenius_energies, molar_change_matrix):
    log_conc = jnp.log(jnp.abs(state) + log_offset)
    log_rate = log_arrhenius_factor[:, None] + jnp.dot(kinetic_exponents, log_conc, precision=maximal_load) - arrhenius_energies[:, None] * inverse_theta
    reaction_rate = jnp.exp(jnp.minimum(log_rate, rate_ceiling))
    return jnp.dot(molar_change_matrix, reaction_rate, precision=maximal_load)

def combust_patches(patches, thermal_values, log_arrhenius_factor, kinetic_exponents, arrhenius_energies, molar_change_matrix, cooling_by_component):
    patch_total, species_count, patch_points = patches.shape
    beginning = patches.transpose(1, 0, 2).reshape(species_count, patch_total * patch_points)
    inverse_theta = (1.0 / thermal_values).reshape(1, patch_total * patch_points)
    rhs = partial(production, inverse_theta=inverse_theta, log_arrhenius_factor=log_arrhenius_factor, kinetic_exponents=kinetic_exponents, arrhenius_energies=arrhenius_energies, molar_change_matrix=molar_change_matrix)
    first = rhs(beginning)
    second = rhs(beginning + 0.5 * chem_step * first)
    third = rhs(beginning + 0.5 * chem_step * second)
    fourth = rhs(beginning + chem_step * third)
    concluding = beginning + chem_step / 6.0 * (first + 2.0 * second + 2.0 * third + fourth)
    thermal_result = thermal_values - jnp.dot(cooling_by_component, concluding - beginning, precision=maximal_load).reshape(patch_total, patch_points)
    return (concluding.reshape(species_count, patch_total, patch_points).transpose(1, 0, 2), thermal_result)

def reference(component_levels, thermal_field, reciprocal_pair_diffusivity, log_arrhenius_factor, kinetic_exponents, arrhenius_energies, molar_change_matrix, cooling_by_component, burning_flags):
    blended_spreading_rate = blend_mean(component_levels, thermal_field, reciprocal_pair_diffusivity)
    time_step = courant / jnp.max(blended_spreading_rate)
    edges = ((1, 1), (0, 0), (1, 1))
    diffused = diffuse(jnp.pad(component_levels, edges), jnp.pad(blended_spreading_rate, edges), time_step)
    species_count = component_levels.shape[1]
    whole_patches = diffused.reshape(LEADING_POINTS, species_count, N_CHEM, PATCH_POINTS).transpose(0, 2, 1, 3).reshape(LEADING_POINTS * N_CHEM, species_count, PATCH_POINTS)
    patchwise_thermal = thermal_field.reshape(LEADING_POINTS * N_CHEM, PATCH_POINTS)
    patch_grand_total = AVG * N_FLOW * N_CHEM
    enumerated = jnp.argsort(1 - burning_flags.reshape(-1), stable=True)[:patch_grand_total].astype(jnp.int32)

    def one_group(picked_patches):
        return combust_patches(whole_patches[picked_patches], patchwise_thermal[picked_patches], log_arrhenius_factor, kinetic_exponents, arrhenius_energies, molar_change_matrix, cooling_by_component)
    new_blocks, fresh_thermal = lax.map(one_group, enumerated.reshape(-1, AVG))
    whole_patches = whole_patches.at[enumerated].set(new_blocks.reshape(patch_grand_total, species_count, PATCH_POINTS))
    patchwise_thermal = patchwise_thermal.at[enumerated].set(fresh_thermal.reshape(patch_grand_total, PATCH_POINTS))
    advanced_components = whole_patches.reshape(LEADING_POINTS, N_CHEM, species_count, PATCH_POINTS).transpose(0, 2, 1, 3).reshape(LEADING_POINTS, species_count, TRAILING_POINTS)
    return (advanced_components, patchwise_thermal.reshape(LEADING_POINTS, TRAILING_POINTS))
```

```python
from functools import partial
import math

import jax
import jax.numpy as jnp
from jax import lax
from jax.experimental import pallas as pl
from jax.experimental.pallas import tpu as pltpu
from jax.sharding import PartitionSpec as P

MESH = pl.DeviceIdType.MESH
F32 = jnp.float32
BF16 = jnp.bfloat16
courant = 0.2
chem_step = 0.05
log_offset = 0.001
rate_ceiling = 2.0
LOG2E = 1.0 / math.log(2.0)
CHUNK = 8
GROUP = 2


def split(x):
    hi = x.astype(BF16)
    return hi, (x - hi.astype(F32)).astype(BF16)


def flux_kernel(
    flow_n, chem_n, c_hbm, t_ref, rr_ref, f_hbm, dt_ref,
    cv, cx, dx, fv, col_out, col_in, peak, in_sem, out_sem, halo_send, halo_recv, max_send, max_recv,
):
    rows, species, lanes = cv.shape
    padded = cx.shape[1]
    chunks = rows // CHUNK
    fi, ci = lax.axis_index("flow"), lax.axis_index("chem")

    def chunk_in(k):
        at = pl.ds(k * CHUNK, CHUNK)
        return pltpu.make_async_copy(c_hbm.at[at], cv.at[at], in_sem.at[k])

    def chunk_out(k):
        at = pl.ds(k * CHUNK, CHUNK)
        return pltpu.make_async_copy(fv.at[at], f_hbm.at[at], out_sem.at[k])

    @pl.loop(0, chunks)
    def _(k):
        chunk_in(k).start()

    barrier = pltpu.get_barrier_semaphore()
    for k in range(1, flow_n):
        pl.semaphore_signal(barrier, inc=1, device_id=(lax.rem(fi + k, flow_n), ci), device_id_type=MESH)
    for k in range(1, chem_n):
        pl.semaphore_signal(barrier, inc=1, device_id=(fi, lax.rem(ci + k, chem_n)), device_id_type=MESH)

    lane = lax.broadcasted_iota(jnp.int32, (padded, lanes), 1)
    ones = jnp.ones((padded, lanes), F32)

    def prepare(x, cols):
        heads, tails = cols

        @pl.when(lax.rem(x, CHUNK) == 0)
        def _():
            chunk_in(x // CHUNK).wait()

        cx[x + 1, 0:species, :] = cv[x]
        cx[x + 1, species : species + 1, :] = t_ref[pl.ds(x, 1), :]
        row = cx[x + 1]
        head_at = lax.rem(2 * x + lanes - 1, lanes)
        heads = jnp.where(lane == head_at, pltpu.roll(row, head_at, 1), heads)
        tails = jnp.where(lane == 2 * x, pltpu.roll(row, lax.rem(2 * x + 1, lanes), 1), tails)
        return heads, tails

    heads, tails = lax.fori_loop(0, rows, prepare, (ones, ones))
    col_out[0] = heads
    col_out[1] = tails
    pl.semaphore_wait(barrier, flow_n + chem_n - 2)

    before, after = lax.rem(fi + flow_n - 1, flow_n), lax.rem(fi + 1, flow_n)
    west, east = lax.rem(ci + chem_n - 1, chem_n), lax.rem(ci + 1, chem_n)

    def halo(k, src, dst, device):
        return pltpu.make_async_remote_copy(
            src_ref=src, dst_ref=dst, send_sem=halo_send.at[k], recv_sem=halo_recv.at[k],
            device_id=device, device_id_type=MESH,
        )

    halos = [
        halo(0, cx.at[1], cx.at[rows + 1], (before, ci)),
        halo(1, cx.at[rows], cx.at[0], (after, ci)),
        halo(2, col_out.at[0], col_in.at[1], (fi, west)),
        halo(3, col_out.at[1], col_in.at[0], (fi, east)),
    ]
    for copy in halos:
        copy.start()

    def spreading(block):
        hi, lo = split(block)
        total = jnp.dot(rr_ref[...], jnp.concatenate([hi, lo], axis=0), preferred_element_type=F32)
        heat = block[species : species + 1, :]
        return heat * jnp.sqrt(heat) / (total[:padded] + total[padded:])

    def pair(p, top):
        d = spreading(jnp.concatenate([cx[2 * p + 1], cx[2 * p + 2]], axis=1))
        dx[2 * p + 1] = d[:, :lanes]
        dx[2 * p + 2] = d[:, lanes:]
        m = jnp.maximum(d[:, :lanes], d[:, lanes:])
        for s in range(0, padded, 8):
            top = jnp.maximum(top, m[s : s + 8])
        return top

    peak[0] = lax.fori_loop(0, rows // 2, pair, jnp.zeros((8, lanes), F32))

    def spread_max(base, count, who):
        return [
            pltpu.make_async_remote_copy(
                src_ref=peak.at[base], dst_ref=peak.at[base + k],
                send_sem=max_send.at[base + k], recv_sem=max_recv.at[base + k],
                device_id=who(k), device_id_type=MESH,
            )
            for k in range(1, count)
        ]

    first = spread_max(0, flow_n, lambda k: (lax.rem(fi + k, flow_n), ci))
    for copy in first:
        copy.start()

    for copy in halos:
        copy.wait()
    zero = jnp.zeros((padded, lanes), F32)
    d = spreading(jnp.concatenate([cx[0], cx[rows + 1]], axis=1))
    dx[0] = jnp.where(fi == 0, zero, d[:, :lanes])
    dx[rows + 1] = jnp.where(fi == flow_n - 1, zero, d[:, lanes:])
    cx[0] = jnp.where(fi == 0, zero, cx[0])
    cx[rows + 1] = jnp.where(fi == flow_n - 1, zero, cx[rows + 1])
    side = jnp.where(lax.rem(lane, 2) == 0, col_in[0], col_in[1])
    d = spreading(side)
    outside = (lax.rem(lane, 2) == 0) & (ci == 0) | (lax.rem(lane, 2) == 1) & (ci == chem_n - 1)
    col_in[0] = jnp.where(outside, zero, side)
    col_in[1] = jnp.where(outside, zero, d)

    def flux_row(x, above):
        c0, d0 = cx[x + 1], dx[x + 1]
        below = (dx[x + 2] + d0) * (cx[x + 2] - c0)
        turn = lax.rem(lanes - 2 * x, lanes)
        side_c = pltpu.roll(col_in[0], turn, 1)
        side_d = pltpu.roll(col_in[1], turn, 1)
        left_c = jnp.where(lane == 0, side_c, pltpu.roll(c0, 1, 1))
        left_d = jnp.where(lane == 0, side_d, pltpu.roll(d0, 1, 1))
        left = (left_d + d0) * (c0 - left_c)
        right = jnp.where(lane == lanes - 1, (side_d + d0) * (side_c - c0), pltpu.roll(left, lanes - 1, 1))
        fv[x] = 0.5 * ((below - above) + (right - left))
        return below

    def flux_chunk(k, above):
        for j in range(CHUNK):
            above = flux_row(k * CHUNK + j, above)
        chunk_out(k).start()
        return above

    above = (dx[0] + dx[1]) * (cx[1] - cx[0])
    above = lax.fori_loop(0, chunks // 2, flux_chunk, above)

    for copy in first:
        copy.wait()
    top = peak[0]
    for k in range(1, flow_n):
        top = jnp.maximum(top, peak[k])
    peak[flow_n] = top
    second = spread_max(flow_n, chem_n, lambda k: (fi, lax.rem(ci + k, chem_n)))
    for copy in second:
        copy.start()
    lax.fori_loop(chunks // 2, chunks, flux_chunk, above)
    for copy in second:
        copy.wait()
    for k in range(1, chem_n):
        top = jnp.maximum(top, peak[flow_n + k])
    dt_ref[...] = courant / jnp.broadcast_to(jnp.max(jnp.max(top, axis=1, keepdims=True), axis=0, keepdims=True), dt_ref.shape)

    @pl.loop(0, chunks)
    def _(k):
        chunk_out(k).wait()


def burn_kernel(
    flag_ref, c_hbm, f_hbm, t_ref, dt_ref, k_ref, m_ref, o_hbm, to_ref,
    cv, fv, xs, base, rate, place, c_sem, f_sem, o_sem,
):
    rows, species, lanes = cv.shape
    padded = fv.shape[1]
    chunks = rows // CHUNK
    width = GROUP * lanes

    def chunk_c(k):
        at = pl.ds(k * CHUNK, CHUNK)
        return pltpu.make_async_copy(c_hbm.at[at], cv.at[at], c_sem.at[k])

    def chunk_f(k):
        at = pl.ds(k * CHUNK, CHUNK)
        return pltpu.make_async_copy(f_hbm.at[at], fv.at[at], f_sem.at[k])

    def row_out(x):
        return pltpu.make_async_copy(cv.at[x], o_hbm.at[x], o_sem)

    @pl.loop(0, chunks)
    def _(k):
        chunk_c(k).start()
        chunk_f(k).start()

    to_ref[...] = t_ref[...]

    def listed(x, count):
        place[count] = x
        return count + flag_ref[x, 0]

    count = lax.fori_loop(0, rows, listed, jnp.int32(0))
    last = place[jnp.maximum(count - 1, 0)]
    for j in range(GROUP):
        place[count + j] = last

    step = dt_ref[0:1, :]

    @pl.loop(0, chunks)
    def _(k):
        chunk_c(k).wait()
        chunk_f(k).wait()
        for j in range(CHUNK):
            x = k * CHUNK + j
            cv[x] = cv[x] + step * fv[x, 0:species, :]

            @pl.when(flag_ref[x, 0] == 0)
            def _():
                row_out(x).start()

    row = lax.broadcasted_iota(jnp.int32, (padded, width), 0)
    extra = lax.broadcasted_iota(jnp.int32, (k_ref.shape[1] // 2 - padded, width), 0)
    ceiling = rate_ceiling * LOG2E

    @pl.loop(0, (count + GROUP - 1) // GROUP)
    def _(g):
        for j in range(GROUP):
            x = place[g * GROUP + j]
            at = slice(j * lanes, (j + 1) * lanes)
            xs[0:species, at] = cv[x]
            xs[species : species + 1, at] = t_ref[pl.ds(x, 1), :]
        x0 = xs[...]
        log1 = jnp.log(jnp.abs(x0) + log_offset)
        inverse = 1.0 / x0[species : species + 1, :]
        full = jnp.concatenate(
            [jnp.where(row == species, 1.0, log1), jnp.where(extra == 0, inverse, 0.0)], axis=0
        )
        hi, lo = split(full)
        terms = jnp.concatenate(
            [jnp.concatenate([hi, hi], axis=0), jnp.concatenate([lo, lo], axis=0)], axis=1
        )
        both = jnp.dot(k_ref[...], terms, preferred_element_type=F32)
        level = both[:, :width] + both[:, width:]
        base[...] = level
        r = jnp.exp2(jnp.minimum(level, ceiling))
        rate[...] = r
        hi, lo = split(r)
        wide = jnp.dot(m_ref[...], hi, preferred_element_type=F32)
        first = wide[:padded] + wide[padded:] + jnp.dot(m_ref[0:padded, :], lo, preferred_element_type=F32)

        def later(state):
            change = jnp.where(row == species, 0.0, jnp.log(jnp.abs(state) + log_offset) - log1)
            change = jnp.concatenate([change, jnp.zeros(extra.shape, F32)], axis=0).astype(BF16)
            level = base[...] + jnp.dot(
                k_ref[:, 0 : k_ref.shape[1] // 2], change, preferred_element_type=F32
            )
            r = jnp.exp2(jnp.minimum(level, ceiling))
            return first + jnp.dot(
                m_ref[0:padded, :], (r - rate[...]).astype(BF16), preferred_element_type=F32
            )

        second = later(x0 + (0.5 * chem_step) * first)
        total = first + 2.0 * second
        third = later(x0 + (0.5 * chem_step) * second)
        total = total + 2.0 * third
        total = total + later(x0 + chem_step * third)
        xs[...] = x0 + (chem_step / 6.0) * total
        for j in range(GROUP):
            x = place[g * GROUP + j]
            at = slice(j * lanes, (j + 1) * lanes)

            @pl.when(g * GROUP + j < count)
            def _():
                cv[x] = xs[0:species, at]
                to_ref[pl.ds(x, 1), :] = xs[species : species + 1, at]
                row_out(x).start()

    pltpu.make_async_copy(cv, o_hbm, o_sem).wait()


def halves(x):
    hi = lax.reduce_precision(x, 8, 7)
    return hi.astype(BF16), (x - hi).astype(BF16)


def per_device(
    flow_n, chem_n,
    component_levels, thermal_field, reciprocal_pair_diffusivity, log_arrhenius_factor,
    kinetic_exponents, arrhenius_energies, molar_change_matrix, cooling_by_component, burning_flags,
):
    rows, species, lanes = component_levels.shape
    reactions = kinetic_exponents.shape[0]
    padded = (species + 16) // 16 * 16
    depth = (padded + 1 + 127) // 128 * 128
    chunks = rows // CHUNK

    pairs = jnp.pad(reciprocal_pair_diffusivity, ((0, padded - species), (0, 0)), constant_values=1.0)
    pairs = jnp.pad(pairs, ((0, 0), (0, padded - species)))
    hi, lo = halves(pairs)
    pairs = jnp.concatenate([jnp.concatenate([hi, hi], 1), jnp.concatenate([lo, lo], 1)], 0)

    orders = jnp.concatenate(
        [
            kinetic_exponents,
            log_arrhenius_factor[:, None],
            jnp.zeros((reactions, padded - species - 1), F32),
            -arrhenius_energies[:, None],
            jnp.zeros((reactions, depth - padded - 1), F32),
        ],
        axis=1,
    ) * LOG2E
    orders = jnp.concatenate(halves(orders), axis=1)

    cooling = jnp.dot(cooling_by_component, molar_change_matrix, precision=lax.Precision.HIGHEST)
    changes = jnp.concatenate(
        [molar_change_matrix, -cooling[None], jnp.zeros((padded - species - 1, reactions), F32)], axis=0
    )
    changes = jnp.concatenate(halves(changes), axis=0)

    vmem = pl.BlockSpec(memory_space=pltpu.VMEM)
    smem = pl.BlockSpec(memory_space=pltpu.SMEM)
    anywhere = pl.BlockSpec(memory_space=pl.ANY)
    flux, step = pl.pallas_call(
        partial(flux_kernel, flow_n, chem_n),
        out_shape=(
            jax.ShapeDtypeStruct((rows, padded, lanes), F32),
            jax.ShapeDtypeStruct((8, lanes), F32),
        ),
        in_specs=[anywhere, vmem, vmem],
        out_specs=(anywhere, vmem),
        scratch_shapes=[
            pltpu.VMEM((rows, species, lanes), F32),
            pltpu.VMEM((rows + 2, padded, lanes), F32),
            pltpu.VMEM((rows + 2, padded, lanes), F32),
            pltpu.VMEM((rows, padded, lanes), F32),
            pltpu.VMEM((2, padded, lanes), F32),
            pltpu.VMEM((2, padded, lanes), F32),
            pltpu.VMEM((flow_n + chem_n, 8, lanes), F32),
            pltpu.SemaphoreType.DMA((chunks,)),
            pltpu.SemaphoreType.DMA((chunks,)),
            pltpu.SemaphoreType.DMA((4,)),
            pltpu.SemaphoreType.DMA((4,)),
            pltpu.SemaphoreType.DMA((flow_n + chem_n,)),
            pltpu.SemaphoreType.DMA((flow_n + chem_n,)),
        ],
        compiler_params=pltpu.CompilerParams(
            collective_id=0, has_side_effects=True, vmem_limit_bytes=40 * 2**20
        ),
        name="flux",
    )(component_levels, thermal_field, pairs)

    return pl.pallas_call(
        burn_kernel,
        out_shape=(
            jax.ShapeDtypeStruct((rows, species, lanes), F32),
            jax.ShapeDtypeStruct((rows, lanes), F32),
        ),
        in_specs=[smem, anywhere, anywhere, vmem, vmem, vmem, vmem],
        out_specs=(anywhere, vmem),
        scratch_shapes=[
            pltpu.VMEM((rows, species, lanes), F32),
            pltpu.VMEM((rows, padded, lanes), F32),
            pltpu.VMEM((padded, GROUP * lanes), F32),
            pltpu.VMEM((reactions, GROUP * lanes), F32),
            pltpu.VMEM((reactions, GROUP * lanes), F32),
            pltpu.SMEM((rows + GROUP,), jnp.int32),
            pltpu.SemaphoreType.DMA((chunks,)),
            pltpu.SemaphoreType.DMA((chunks,)),
            pltpu.SemaphoreType.DMA(()),
        ],
        compiler_params=pltpu.CompilerParams(vmem_limit_bytes=48 * 2**20),
        name="burn",
    )(burning_flags, component_levels, flux, thermal_field, step, orders, changes)


def solution(mesh):
    placed = (
        P("flow", None, "chem"),
        P("flow", "chem"),
        P(),
        P(),
        P(),
        P(),
        P(),
        P(),
        P("flow", "chem"),
    )
    return jax.shard_map(
        partial(per_device, mesh.shape["flow"], mesh.shape["chem"]),
        mesh=mesh,
        in_specs=placed,
        out_specs=(P("flow", None, "chem"), P("flow", "chem")),
        check_vma=False,
    )
```

```python
from functools import partial
import math

import jax
import jax.numpy as jnp
from jax import lax
from jax.experimental import pallas as pl
from jax.experimental.pallas import tpu as pltpu
from jax.sharding import PartitionSpec as P

MESH = pl.DeviceIdType.MESH
F32 = jnp.float32
BF16 = jnp.bfloat16
courant = 0.2
chem_step = 0.05
log_offset = 0.001
rate_ceiling = 2.0
LOG2E = 1.0 / math.log(2.0)
CHUNK = 8
GROUP = 4
VMEM_BYTES = 56 * 2**20


def split(x):
    hi = x.astype(BF16)
    return hi, (x - hi.astype(F32)).astype(BF16)


def row_copies(start, k, species_hbm, rows_vmem, sem):
    for j in range(CHUNK):
        x = k * CHUNK + j
        copy = pltpu.make_async_copy(species_hbm.at[:, x], rows_vmem.at[x], sem.at[x])
        if start:
            copy.start()
        else:
            copy.wait()


def flux_kernel(
    flow_n, chem_n, c_hbm, t_ref, pair_ref, f_hbm, dt_ref,
    cv, cx, dx, fv, pairs, rr_ref, col_out, col_in, peak,
    in_sem, out_sem, halo_send, halo_recv, max_send, max_recv,
):
    rows, species, lanes = cv.shape
    padded = cx.shape[1]
    depth = pairs.shape[1]
    chunks = rows // CHUNK
    fi, ci = lax.axis_index("flow"), lax.axis_index("chem")

    def chunk_out(k):
        at = pl.ds(k * CHUNK, CHUNK)
        return pltpu.make_async_copy(fv.at[at], f_hbm.at[at], out_sem.at[k])

    @pl.loop(0, chunks)
    def _(k):
        row_copies(True, k, c_hbm, cv, in_sem)

    barrier = pltpu.get_barrier_semaphore()
    for k in range(1, flow_n):
        pl.semaphore_signal(barrier, inc=1, device_id=(lax.rem(fi + k, flow_n), ci), device_id_type=MESH)
    for k in range(1, chem_n):
        pl.semaphore_signal(barrier, inc=1, device_id=(fi, lax.rem(ci + k, chem_n)), device_id_type=MESH)

    at_col = lax.broadcasted_iota(jnp.int32, pairs.shape, 1)
    pairs[...] = jnp.where(at_col < species, 1.0, 0.0)
    pairs[0:species, 0:species] = pair_ref[...]
    hi, lo = split(pairs[...])
    rr_ref[...] = jnp.concatenate(
        [jnp.concatenate([hi, hi], axis=1), jnp.concatenate([lo, lo], axis=1)], axis=0
    )

    lane = lax.broadcasted_iota(jnp.int32, (padded, lanes), 1)
    ones = jnp.ones((padded, lanes), F32)

    def prepare(k, cols):
        heads, tails = cols
        row_copies(False, k, c_hbm, cv, in_sem)
        for j in range(CHUNK):
            x = k * CHUNK + j
            cx[x + 1, 0:species, :] = cv[x]
            cx[x + 1, species : species + 1, :] = t_ref[pl.ds(x, 1), :]
        for j in range(CHUNK):
            x = k * CHUNK + j
            row = cx[x + 1]
            head_at = lax.rem(2 * x + lanes - 1, lanes)
            heads = jnp.where(lane == head_at, pltpu.roll(row, head_at, 1), heads)
            tails = jnp.where(lane == 2 * x, pltpu.roll(row, lax.rem(2 * x + 1, lanes), 1), tails)
        return heads, tails

    heads, tails = lax.fori_loop(0, chunks, prepare, (ones, ones))
    col_out[0] = heads
    col_out[1] = tails
    pl.semaphore_wait(barrier, flow_n + chem_n - 2)

    before, after = lax.rem(fi + flow_n - 1, flow_n), lax.rem(fi + 1, flow_n)
    west, east = lax.rem(ci + chem_n - 1, chem_n), lax.rem(ci + 1, chem_n)

    def halo(k, src, dst, device):
        return pltpu.make_async_remote_copy(
            src_ref=src, dst_ref=dst, send_sem=halo_send.at[k], recv_sem=halo_recv.at[k],
            device_id=device, device_id_type=MESH,
        )

    halos = [
        halo(0, cx.at[1], cx.at[rows + 1], (before, ci)),
        halo(1, cx.at[rows], cx.at[0], (after, ci)),
        halo(2, col_out.at[0], col_in.at[1], (fi, west)),
        halo(3, col_out.at[1], col_in.at[0], (fi, east)),
    ]
    for copy in halos:
        copy.start()

    def spreading(block):
        hi, lo = split(block)
        blank = jnp.zeros((depth - padded, block.shape[1]), BF16)
        total = jnp.dot(
            rr_ref[...], jnp.concatenate([hi, blank, lo, blank], axis=0), preferred_element_type=F32
        )
        heat = block[species : species + 1, :]
        return heat * jnp.sqrt(heat) / (total[:padded] + total[padded:])

    def diffusivities(k, top):
        first = k * CHUNK + 1
        d = spreading(jnp.concatenate([cx[first + j] for j in range(CHUNK)], axis=1))
        m = d[:, :lanes]
        for j in range(CHUNK):
            here = d[:, j * lanes : (j + 1) * lanes]
            dx[first + j] = here
            m = jnp.maximum(m, here)
        for s in range(0, padded, 8):
            top = jnp.maximum(top, m[s : s + 8])
        return top

    peak[0] = lax.fori_loop(0, chunks, diffusivities, jnp.zeros((8, lanes), F32))

    def spread_max(base, count, who):
        return [
            pltpu.make_async_remote_copy(
                src_ref=peak.at[base], dst_ref=peak.at[base + k],
                send_sem=max_send.at[base + k], recv_sem=max_recv.at[base + k],
                device_id=who(k), device_id_type=MESH,
            )
            for k in range(1, count)
        ]

    first = spread_max(0, flow_n, lambda k: (lax.rem(fi + k, flow_n), ci))
    for copy in first:
        copy.start()

    for copy in halos:
        copy.wait()
    zero = jnp.zeros((padded, lanes), F32)
    side = jnp.where(lax.rem(lane, 2) == 0, col_in[0], col_in[1])
    d = spreading(jnp.concatenate([cx[0], cx[rows + 1], side], axis=1))
    dx[0] = jnp.where(fi == 0, zero, d[:, :lanes])
    dx[rows + 1] = jnp.where(fi == flow_n - 1, zero, d[:, lanes : 2 * lanes])
    cx[0] = jnp.where(fi == 0, zero, cx[0])
    cx[rows + 1] = jnp.where(fi == flow_n - 1, zero, cx[rows + 1])
    outside = (lax.rem(lane, 2) == 0) & (ci == 0) | (lax.rem(lane, 2) == 1) & (ci == chem_n - 1)
    col_in[0] = jnp.where(outside, zero, side)
    col_in[1] = jnp.where(outside, zero, d[:, 2 * lanes :])

    at_lane = lax.broadcasted_iota(jnp.int32, (8, lanes), 1)

    def flux_chunk(k):
        for s in range(0, padded, 8):
            at = slice(s, s + 8)
            x = k * CHUNK
            c0, d0 = cx[x + 1, at, :], dx[x + 1, at, :]
            above = (dx[x, at, :] + d0) * (c0 - cx[x, at, :])
            for j in range(CHUNK):
                x = k * CHUNK + j
                c1, d1 = cx[x + 2, at, :], dx[x + 2, at, :]
                below = (d1 + d0) * (c1 - c0)
                turn = lax.rem(lanes - 2 * x, lanes)
                side_c = pltpu.roll(col_in[0, at, :], turn, 1)
                side_d = pltpu.roll(col_in[1, at, :], turn, 1)
                left_c = jnp.where(at_lane == 0, side_c, pltpu.roll(c0, 1, 1))
                left_d = jnp.where(at_lane == 0, side_d, pltpu.roll(d0, 1, 1))
                left = (left_d + d0) * (c0 - left_c)
                right = jnp.where(
                    at_lane == lanes - 1, (side_d + d0) * (side_c - c0), pltpu.roll(left, lanes - 1, 1)
                )
                fv[x, at, :] = 0.5 * ((below - above) + (right - left))
                c0, d0, above = c1, d1, below
        chunk_out(k).start()

    pl.loop(0, chunks // 2)(flux_chunk)

    for copy in first:
        copy.wait()
    top = peak[0]
    for k in range(1, flow_n):
        top = jnp.maximum(top, peak[k])
    peak[flow_n] = top
    second = spread_max(flow_n, chem_n, lambda k: (fi, lax.rem(ci + k, chem_n)))
    for copy in second:
        copy.start()
    pl.loop(chunks // 2, chunks)(flux_chunk)
    for copy in second:
        copy.wait()
    for k in range(1, chem_n):
        top = jnp.maximum(top, peak[flow_n + k])
    dt_ref[...] = courant / jnp.broadcast_to(
        jnp.max(jnp.max(top, axis=1, keepdims=True), axis=0, keepdims=True), dt_ref.shape
    )

    @pl.loop(0, chunks)
    def _(k):
        chunk_out(k).wait()


def burn_kernel(
    flag_ref, c_hbm, f_hbm, t_ref, dt_ref, factor_ref, order_ref, energy_ref, change_ref, cool_ref,
    o_hbm, to_ref,
    cv, fv, xs, base, rate, wide_k, side_k, wide_m, k_ref, m_ref, place, c_sem, f_sem, o_sem,
):
    rows, species, lanes = cv.shape
    padded = fv.shape[1]
    depth = wide_k.shape[1]
    reactions = wide_k.shape[0]
    chunks = rows // CHUNK
    width = GROUP * lanes

    def chunk_f(k):
        at = pl.ds(k * CHUNK, CHUNK)
        return pltpu.make_async_copy(f_hbm.at[at], fv.at[at], f_sem.at[k])

    def row_out(x):
        return pltpu.make_async_copy(cv.at[x], o_hbm.at[:, x], o_sem)

    @pl.loop(0, chunks)
    def _(k):
        row_copies(True, k, c_hbm, cv, c_sem)
        chunk_f(k).start()

    to_ref[...] = t_ref[...]

    def listed(x, count):
        place[count] = x
        return count + flag_ref[0, x]

    count = lax.fori_loop(0, rows, listed, jnp.int32(0))
    last = place[jnp.maximum(count - 1, 0)]
    for j in range(GROUP):
        place[count + j] = last

    wide_k[...] = jnp.zeros(wide_k.shape, F32)
    wide_k[:, 0:species] = order_ref[...]
    side_k[...] = jnp.zeros(side_k.shape, F32)
    side_k[species : species + 1, 0:reactions] = factor_ref[...]
    side_k[padded : padded + 1, 0:reactions] = -energy_ref[...]
    hi, lo = split((wide_k[...] + side_k[...].T[0:reactions, :]) * LOG2E)
    k_ref[:, 0:depth] = hi
    k_ref[:, depth:] = lo
    cooled = jnp.dot(
        jnp.broadcast_to(cool_ref[...], (8, species)), change_ref[...],
        precision=lax.Precision.HIGHEST, preferred_element_type=F32,
    )
    wide_m[...] = jnp.zeros(wide_m.shape, F32)
    wide_m[0:species, :] = change_ref[...]
    wide_m[species : species + 1, :] = -cooled[0:1]
    hi, lo = split(wide_m[...])
    m_ref[0:padded, :] = hi
    m_ref[padded:, :] = lo

    step = dt_ref[0:1, :]

    @pl.loop(0, chunks)
    def _(k):
        row_copies(False, k, c_hbm, cv, c_sem)
        chunk_f(k).wait()
        for j in range(CHUNK):
            x = k * CHUNK + j
            cv[x] = cv[x] + step * fv[x, 0:species, :]
        for j in range(CHUNK):
            x = k * CHUNK + j

            @pl.when(flag_ref[0, x] == 0)
            def _():
                row_out(x).start()

    row = lax.broadcasted_iota(jnp.int32, (padded, width), 0)
    extra = lax.broadcasted_iota(jnp.int32, (k_ref.shape[1] // 2 - padded, width), 0)
    ceiling = rate_ceiling * LOG2E

    @pl.loop(0, (count + GROUP - 1) // GROUP)
    def _(g):
        for j in range(GROUP):
            x = place[g * GROUP + j]
            at = slice(j * lanes, (j + 1) * lanes)
            xs[0:species, at] = cv[x]
            xs[species : species + 1, at] = t_ref[pl.ds(x, 1), :]
        x0 = xs[...]
        log1 = jnp.log(jnp.abs(x0) + log_offset)
        inverse = 1.0 / x0[species : species + 1, :]
        full = jnp.concatenate(
            [jnp.where(row == species, 1.0, log1), jnp.where(extra == 0, inverse, 0.0)], axis=0
        )
        hi, lo = split(full)
        terms = jnp.concatenate(
            [jnp.concatenate([hi, hi], axis=0), jnp.concatenate([lo, lo], axis=0)], axis=1
        )
        both = jnp.dot(k_ref[...], terms, preferred_element_type=F32)
        level = both[:, :width] + both[:, width:]
        base[...] = level
        r = jnp.exp2(jnp.minimum(level, ceiling))
        rate[...] = r
        hi, lo = split(r)
        wide = jnp.dot(m_ref[...], hi, preferred_element_type=F32)
        first = wide[:padded] + wide[padded:] + jnp.dot(m_ref[0:padded, :], lo, preferred_element_type=F32)

        def later(state):
            change = jnp.where(row == species, 0.0, jnp.log(jnp.abs(state) + log_offset) - log1)
            change = jnp.concatenate([change, jnp.zeros(extra.shape, F32)], axis=0).astype(BF16)
            level = base[...] + jnp.dot(
                k_ref[:, 0 : k_ref.shape[1] // 2], change, preferred_element_type=F32
            )
            r = jnp.exp2(jnp.minimum(level, ceiling))
            return first + jnp.dot(
                m_ref[0:padded, :], (r - rate[...]).astype(BF16), preferred_element_type=F32
            )

        second = later(x0 + (0.5 * chem_step) * first)
        total = first + 2.0 * second
        third = later(x0 + (0.5 * chem_step) * second)
        total = total + 2.0 * third
        total = total + later(x0 + chem_step * third)
        xs[...] = x0 + (chem_step / 6.0) * total
        for j in range(GROUP):
            x = place[g * GROUP + j]
            at = slice(j * lanes, (j + 1) * lanes)

            @pl.when(g * GROUP + j < count)
            def _():
                cv[x] = xs[0:species, at]
                to_ref[pl.ds(x, 1), :] = xs[species : species + 1, at]
                row_out(x).start()

    @pl.loop(0, rows)
    def _(x):
        row_out(x).wait()


def per_device(
    flow_n, chem_n,
    component_levels, thermal_field, reciprocal_pair_diffusivity, log_arrhenius_factor,
    kinetic_exponents, arrhenius_energies, molar_change_matrix, cooling_by_component, burning_flags,
):
    rows, species, lanes = component_levels.shape
    reactions = kinetic_exponents.shape[0]
    padded = (species + 16) // 16 * 16
    depth = (padded + 1 + 127) // 128 * 128
    chunks = rows // CHUNK

    levels = component_levels.transpose(1, 0, 2)
    vmem = pl.BlockSpec(memory_space=pltpu.VMEM)
    smem = pl.BlockSpec(memory_space=pltpu.SMEM)
    anywhere = pl.BlockSpec(memory_space=pl.ANY)
    flux, step = pl.pallas_call(
        partial(flux_kernel, flow_n, chem_n),
        out_shape=(
            jax.ShapeDtypeStruct((rows, padded, lanes), F32),
            jax.ShapeDtypeStruct((8, lanes), F32),
        ),
        in_specs=[anywhere, vmem, vmem],
        out_specs=(anywhere, vmem),
        scratch_shapes=[
            pltpu.VMEM((rows, species, lanes), F32),
            pltpu.VMEM((rows + 2, padded, lanes), F32),
            pltpu.VMEM((rows + 2, padded, lanes), F32),
            pltpu.VMEM((rows, padded, lanes), F32),
            pltpu.VMEM((padded, depth), F32),
            pltpu.VMEM((2 * padded, 2 * depth), BF16),
            pltpu.VMEM((2, padded, lanes), F32),
            pltpu.VMEM((2, padded, lanes), F32),
            pltpu.VMEM((flow_n + chem_n, 8, lanes), F32),
            pltpu.SemaphoreType.DMA((rows,)),
            pltpu.SemaphoreType.DMA((chunks,)),
            pltpu.SemaphoreType.DMA((4,)),
            pltpu.SemaphoreType.DMA((4,)),
            pltpu.SemaphoreType.DMA((flow_n + chem_n,)),
            pltpu.SemaphoreType.DMA((flow_n + chem_n,)),
        ],
        compiler_params=pltpu.CompilerParams(
            collective_id=0, has_side_effects=True, vmem_limit_bytes=VMEM_BYTES
        ),
        name="flux",
    )(levels, thermal_field, reciprocal_pair_diffusivity)

    advanced, heat = pl.pallas_call(
        burn_kernel,
        out_shape=(
            jax.ShapeDtypeStruct((species, rows, lanes), F32),
            jax.ShapeDtypeStruct((rows, lanes), F32),
        ),
        in_specs=[smem, anywhere, anywhere] + [vmem] * 7,
        out_specs=(anywhere, vmem),
        scratch_shapes=[
            pltpu.VMEM((rows, species, lanes), F32),
            pltpu.VMEM((rows, padded, lanes), F32),
            pltpu.VMEM((padded, GROUP * lanes), F32),
            pltpu.VMEM((reactions, GROUP * lanes), F32),
            pltpu.VMEM((reactions, GROUP * lanes), F32),
            pltpu.VMEM((reactions, depth), F32),
            pltpu.VMEM((depth, (reactions + 127) // 128 * 128), F32),
            pltpu.VMEM((padded, reactions), F32),
            pltpu.VMEM((reactions, 2 * depth), BF16),
            pltpu.VMEM((2 * padded, reactions), BF16),
            pltpu.SMEM((rows + GROUP,), jnp.int32),
            pltpu.SemaphoreType.DMA((rows,)),
            pltpu.SemaphoreType.DMA((chunks,)),
            pltpu.SemaphoreType.DMA(()),
        ],
        compiler_params=pltpu.CompilerParams(vmem_limit_bytes=VMEM_BYTES),
        name="burn",
    )(
        burning_flags.T, levels, flux, thermal_field, step, log_arrhenius_factor[None],
        kinetic_exponents, arrhenius_energies[None], molar_change_matrix, cooling_by_component[None],
    )
    return advanced.transpose(1, 0, 2), heat


def solution(mesh):
    placed = (
        P("flow", None, "chem"),
        P("flow", "chem"),
        P(),
        P(),
        P(),
        P(),
        P(),
        P(),
        P("flow", "chem"),
    )
    return jax.shard_map(
        partial(per_device, mesh.shape["flow"], mesh.shape["chem"]),
        mesh=mesh,
        in_specs=placed,
        out_specs=(P("flow", None, "chem"), P("flow", "chem")),
        check_vma=False,
    )
```

```python
from functools import partial
import math

import jax
import jax.numpy as jnp
from jax import lax
from jax.experimental import pallas as pl
from jax.experimental.pallas import tpu as pltpu
from jax.sharding import PartitionSpec as P

MESH = pl.DeviceIdType.MESH
F32 = jnp.float32
BF16 = jnp.bfloat16
courant = 0.2
chem_step = 0.05
log_offset = 0.001
rate_ceiling = 2.0
LOG2E = 1.0 / math.log(2.0)
CHUNK = 8
GROUP = 8
VMEM_BYTES = 56 * 2**20


def split(x):
    hi = x.astype(BF16)
    return hi, (x - hi.astype(F32)).astype(BF16)


def row_copies(start, k, species_hbm, rows_vmem, sem):
    for j in range(CHUNK):
        x = k * CHUNK + j
        copy = pltpu.make_async_copy(species_hbm.at[:, x], rows_vmem.at[x], sem.at[x])
        if start:
            copy.start()
        else:
            copy.wait()


def flux_kernel(
    flow_n, chem_n, c_hbm, t_ref, pair_ref, f_hbm, dt_ref,
    cv, cx, dx, fv, pairs, rr_ref, col_out, col_in, peak,
    in_sem, out_sem, halo_send, halo_recv, max_send, max_recv,
):
    rows, species, lanes = cv.shape
    padded = cx.shape[1]
    depth = pairs.shape[1]
    chunks = rows // CHUNK
    fi, ci = lax.axis_index("flow"), lax.axis_index("chem")

    def chunk_out(k):
        at = pl.ds(k * CHUNK, CHUNK)
        return pltpu.make_async_copy(fv.at[at], f_hbm.at[at], out_sem.at[k])

    @pl.loop(0, chunks)
    def _(k):
        row_copies(True, k, c_hbm, cv, in_sem)

    barrier = pltpu.get_barrier_semaphore()
    for k in range(1, flow_n):
        pl.semaphore_signal(barrier, inc=1, device_id=(lax.rem(fi + k, flow_n), ci), device_id_type=MESH)
    for k in range(1, chem_n):
        pl.semaphore_signal(barrier, inc=1, device_id=(fi, lax.rem(ci + k, chem_n)), device_id_type=MESH)

    at_col = lax.broadcasted_iota(jnp.int32, pairs.shape, 1)
    pairs[...] = jnp.where(at_col < species, 1.0, 0.0)
    pairs[0:species, 0:species] = pair_ref[...]
    hi, lo = split(pairs[...])
    rr_ref[...] = jnp.concatenate(
        [jnp.concatenate([hi, hi], axis=1), jnp.concatenate([lo, lo], axis=1)], axis=0
    )

    lane = lax.broadcasted_iota(jnp.int32, (padded, lanes), 1)

    def prepare(k, cols):
        row_copies(False, k, c_hbm, cv, in_sem)
        for j in range(CHUNK):
            x = k * CHUNK + j
            cx[x + 1, 0:species, :] = cv[x]
            cx[x + 1, species : species + 1, :] = t_ref[pl.ds(x, 1), :]
        for j in range(CHUNK):
            x = k * CHUNK + j
            edges = pltpu.roll(cx[x + 1], lanes - 1, 1)
            cols = jnp.where(lane >= lanes - 2, edges, pltpu.roll(cols, lanes - 2, 1))
        return cols

    cols = lax.fori_loop(0, chunks, prepare, jnp.ones((padded, lanes), F32))
    cols = pltpu.roll(cols, 2 * rows, 1) if 2 * rows < lanes else cols
    col_out[0] = pltpu.roll(cols, lanes - 2, 1)
    col_out[1] = cols
    pl.semaphore_wait(barrier, flow_n + chem_n - 2)

    before, after = lax.rem(fi + flow_n - 1, flow_n), lax.rem(fi + 1, flow_n)
    west, east = lax.rem(ci + chem_n - 1, chem_n), lax.rem(ci + 1, chem_n)

    def halo(k, src, dst, device):
        return pltpu.make_async_remote_copy(
            src_ref=src, dst_ref=dst, send_sem=halo_send.at[k], recv_sem=halo_recv.at[k],
            device_id=device, device_id_type=MESH,
        )

    halos = [
        halo(0, cx.at[1], cx.at[rows + 1], (before, ci)),
        halo(1, cx.at[rows], cx.at[0], (after, ci)),
        halo(2, col_out.at[0], col_in.at[1], (fi, west)),
        halo(3, col_out.at[1], col_in.at[0], (fi, east)),
    ]
    for copy in halos:
        copy.start()

    def spreading(block):
        hi, lo = split(block)
        blank = jnp.zeros((depth - padded, block.shape[1]), BF16)
        total = jnp.dot(
            rr_ref[...], jnp.concatenate([hi, blank, lo, blank], axis=0), preferred_element_type=F32
        )
        heat = block[species : species + 1, :]
        return heat * jnp.sqrt(heat) / (total[:padded] + total[padded:])

    def diffusivities(k, top):
        first = k * CHUNK + 1
        d = spreading(jnp.concatenate([cx[first + j] for j in range(CHUNK)], axis=1))
        m = d[:, :lanes]
        for j in range(CHUNK):
            here = d[:, j * lanes : (j + 1) * lanes]
            dx[first + j] = here
            m = jnp.maximum(m, here)
        for s in range(0, padded, 8):
            top = jnp.maximum(top, m[s : s + 8])
        return top

    peak[0] = lax.fori_loop(0, chunks, diffusivities, jnp.zeros((8, lanes), F32))

    def spread_max(base, count, who):
        return [
            pltpu.make_async_remote_copy(
                src_ref=peak.at[base], dst_ref=peak.at[base + k],
                send_sem=max_send.at[base + k], recv_sem=max_recv.at[base + k],
                device_id=who(k), device_id_type=MESH,
            )
            for k in range(1, count)
        ]

    first = spread_max(0, flow_n, lambda k: (lax.rem(fi + k, flow_n), ci))
    for copy in first:
        copy.start()

    for copy in halos:
        copy.wait()
    zero = jnp.zeros((padded, lanes), F32)
    side = jnp.where(lax.rem(lane, 2) == 0, col_in[0], col_in[1])
    d = spreading(jnp.concatenate([cx[0], cx[rows + 1], side], axis=1))
    dx[0] = jnp.where(fi == 0, zero, d[:, :lanes])
    dx[rows + 1] = jnp.where(fi == flow_n - 1, zero, d[:, lanes : 2 * lanes])
    cx[0] = jnp.where(fi == 0, zero, cx[0])
    cx[rows + 1] = jnp.where(fi == flow_n - 1, zero, cx[rows + 1])
    outside = (lax.rem(lane, 2) == 0) & (ci == 0) | (lax.rem(lane, 2) == 1) & (ci == chem_n - 1)
    col_in[0] = jnp.where(outside, zero, side)
    col_in[1] = jnp.where(outside, zero, d[:, 2 * lanes :])

    at_lane = lax.broadcasted_iota(jnp.int32, (8, lanes), 1)

    def flux_chunk(k):
        for s in range(0, padded, 8):
            at = slice(s, s + 8)
            x = k * CHUNK
            c0, d0 = cx[x + 1, at, :], dx[x + 1, at, :]
            above = (dx[x, at, :] + d0) * (c0 - cx[x, at, :])
            side_c, side_d = col_in[0, at, :], col_in[1, at, :]
            for j in range(CHUNK):
                x = k * CHUNK + j
                c1, d1 = cx[x + 2, at, :], dx[x + 2, at, :]
                below = (d1 + d0) * (c1 - c0)
                left_c = jnp.where(at_lane == 0, side_c, pltpu.roll(c0, 1, 1))
                left_d = jnp.where(at_lane == 0, side_d, pltpu.roll(d0, 1, 1))
                left = (left_d + d0) * (c0 - left_c)
                right = jnp.where(
                    at_lane == lanes - 1, (side_d + d0) * (side_c - c0), pltpu.roll(left, lanes - 1, 1)
                )
                fv[x, at, :] = 0.5 * ((below - above) + (right - left))
                c0, d0, above = c1, d1, below
                side_c = pltpu.roll(side_c, lanes - 2, 1)
                side_d = pltpu.roll(side_d, lanes - 2, 1)
            col_in[0, at, :] = side_c
            col_in[1, at, :] = side_d
        chunk_out(k).start()

    pl.loop(0, chunks // 2)(flux_chunk)

    for copy in first:
        copy.wait()
    top = peak[0]
    for k in range(1, flow_n):
        top = jnp.maximum(top, peak[k])
    peak[flow_n] = top
    second = spread_max(flow_n, chem_n, lambda k: (fi, lax.rem(ci + k, chem_n)))
    for copy in second:
        copy.start()
    pl.loop(chunks // 2, chunks)(flux_chunk)
    for copy in second:
        copy.wait()
    for k in range(1, chem_n):
        top = jnp.maximum(top, peak[flow_n + k])
    dt_ref[...] = courant / jnp.broadcast_to(
        jnp.max(jnp.max(top, axis=1, keepdims=True), axis=0, keepdims=True), dt_ref.shape
    )

    @pl.loop(0, chunks)
    def _(k):
        chunk_out(k).wait()


def burn_kernel(
    flag_ref, c_hbm, f_hbm, t_ref, dt_ref, factor_ref, order_ref, energy_ref, change_ref, cool_ref,
    o_hbm, to_ref,
    cv, fv, xs, base, rate, wide_k, side_k, wide_m, k_ref, m_ref, place, c_sem, f_sem, o_sem,
):
    rows, species, lanes = cv.shape
    padded = fv.shape[1]
    depth = wide_k.shape[1]
    reactions = wide_k.shape[0]
    chunks = rows // CHUNK
    width = GROUP * lanes

    def chunk_f(k):
        at = pl.ds(k * CHUNK, CHUNK)
        return pltpu.make_async_copy(f_hbm.at[at], fv.at[at], f_sem.at[k])

    def row_out(x):
        return pltpu.make_async_copy(cv.at[x], o_hbm.at[:, x], o_sem)

    @pl.loop(0, chunks)
    def _(k):
        row_copies(True, k, c_hbm, cv, c_sem)
        chunk_f(k).start()

    to_ref[...] = t_ref[...]

    def listed(x, count):
        place[count] = x
        return count + flag_ref[0, x]

    count = lax.fori_loop(0, rows, listed, jnp.int32(0))
    last = place[jnp.maximum(count - 1, 0)]
    for j in range(GROUP):
        place[count + j] = last

    wide_k[...] = jnp.zeros(wide_k.shape, F32)
    wide_k[:, 0:species] = order_ref[...]
    side_k[...] = jnp.zeros(side_k.shape, F32)
    side_k[species : species + 1, 0:reactions] = factor_ref[...].reshape(1, reactions)
    side_k[padded : padded + 1, 0:reactions] = -energy_ref[...].reshape(1, reactions)
    hi, lo = split((wide_k[...] + side_k[...].T[0:reactions, :]) * LOG2E)
    k_ref[:, 0:depth] = hi
    k_ref[:, depth:] = lo
    cooled = jnp.dot(
        jnp.broadcast_to(cool_ref[...], (8, species)), change_ref[...],
        precision=lax.Precision.HIGHEST, preferred_element_type=F32,
    )
    wide_m[...] = jnp.zeros(wide_m.shape, F32)
    wide_m[0:species, :] = change_ref[...]
    wide_m[species : species + 1, :] = -cooled[0:1]
    hi, lo = split(wide_m[...])
    m_ref[0:padded, :] = hi
    m_ref[padded:, :] = lo

    step = dt_ref[0:1, :]

    @pl.loop(0, chunks)
    def _(k):
        row_copies(False, k, c_hbm, cv, c_sem)
        chunk_f(k).wait()
        for j in range(CHUNK):
            x = k * CHUNK + j
            cv[x] = cv[x] + step * fv[x, 0:species, :]
        for j in range(CHUNK):
            x = k * CHUNK + j

            @pl.when(flag_ref[0, x] == 0)
            def _():
                row_out(x).start()

    row = lax.broadcasted_iota(jnp.int32, (padded, width), 0)
    extra = lax.broadcasted_iota(jnp.int32, (k_ref.shape[1] // 2 - padded, width), 0)
    ceiling = rate_ceiling * LOG2E

    @pl.loop(0, (count + GROUP - 1) // GROUP)
    def _(g):
        for j in range(GROUP):
            x = place[g * GROUP + j]
            at = slice(j * lanes, (j + 1) * lanes)
            xs[0:species, at] = cv[x]
            xs[species : species + 1, at] = t_ref[pl.ds(x, 1), :]
        x0 = xs[...]
        log1 = jnp.log(jnp.abs(x0) + log_offset)
        inverse = 1.0 / x0[species : species + 1, :]
        full = jnp.concatenate(
            [jnp.where(row == species, 1.0, log1), jnp.where(extra == 0, inverse, 0.0)], axis=0
        )
        hi, lo = split(full)
        terms = jnp.concatenate(
            [jnp.concatenate([hi, hi], axis=0), jnp.concatenate([lo, lo], axis=0)], axis=1
        )
        both = jnp.dot(k_ref[...], terms, preferred_element_type=F32)
        level = both[:, :width] + both[:, width:]
        base[...] = level
        r = jnp.exp2(jnp.minimum(level, ceiling))
        rate[...] = r
        hi, lo = split(r)
        wide = jnp.dot(m_ref[...], hi, preferred_element_type=F32)
        first = wide[:padded] + wide[padded:] + jnp.dot(m_ref[0:padded, :], lo, preferred_element_type=F32)

        def later(state):
            change = jnp.where(row == species, 0.0, jnp.log(jnp.abs(state) + log_offset) - log1)
            change = jnp.concatenate([change, jnp.zeros(extra.shape, F32)], axis=0).astype(BF16)
            level = base[...] + jnp.dot(
                k_ref[:, 0 : k_ref.shape[1] // 2], change, preferred_element_type=F32
            )
            r = jnp.exp2(jnp.minimum(level, ceiling))
            return first + jnp.dot(
                m_ref[0:padded, :], (r - rate[...]).astype(BF16), preferred_element_type=F32
            )

        second = later(x0 + (0.5 * chem_step) * first)
        total = first + 2.0 * second
        third = later(x0 + (0.5 * chem_step) * second)
        total = total + 2.0 * third
        total = total + later(x0 + chem_step * third)
        xs[...] = x0 + (chem_step / 6.0) * total
        for j in range(GROUP):
            x = place[g * GROUP + j]
            at = slice(j * lanes, (j + 1) * lanes)

            @pl.when(g * GROUP + j < count)
            def _():
                cv[x] = xs[0:species, at]
                to_ref[pl.ds(x, 1), :] = xs[species : species + 1, at]
                row_out(x).start()

    @pl.loop(0, rows)
    def _(x):
        row_out(x).wait()


def per_device(
    flow_n, chem_n,
    component_levels, thermal_field, reciprocal_pair_diffusivity, log_arrhenius_factor,
    kinetic_exponents, arrhenius_energies, molar_change_matrix, cooling_by_component, burning_flags,
):
    rows, species, lanes = component_levels.shape
    reactions = kinetic_exponents.shape[0]
    padded = (species + 16) // 16 * 16
    depth = (padded + 1 + 127) // 128 * 128
    chunks = rows // CHUNK

    levels = component_levels.transpose(1, 0, 2)
    vmem = pl.BlockSpec(memory_space=pltpu.VMEM)
    smem = pl.BlockSpec(memory_space=pltpu.SMEM)
    anywhere = pl.BlockSpec(memory_space=pl.ANY)
    flux, step = pl.pallas_call(
        partial(flux_kernel, flow_n, chem_n),
        out_shape=(
            jax.ShapeDtypeStruct((rows, padded, lanes), F32),
            jax.ShapeDtypeStruct((8, lanes), F32),
        ),
        in_specs=[anywhere, vmem, vmem],
        out_specs=(anywhere, vmem),
        scratch_shapes=[
            pltpu.VMEM((rows, species, lanes), F32),
            pltpu.VMEM((rows + 2, padded, lanes), F32),
            pltpu.VMEM((rows + 2, padded, lanes), F32),
            pltpu.VMEM((rows, padded, lanes), F32),
            pltpu.VMEM((padded, depth), F32),
            pltpu.VMEM((2 * padded, 2 * depth), BF16),
            pltpu.VMEM((2, padded, lanes), F32),
            pltpu.VMEM((2, padded, lanes), F32),
            pltpu.VMEM((flow_n + chem_n, 8, lanes), F32),
            pltpu.SemaphoreType.DMA((rows,)),
            pltpu.SemaphoreType.DMA((chunks,)),
            pltpu.SemaphoreType.DMA((4,)),
            pltpu.SemaphoreType.DMA((4,)),
            pltpu.SemaphoreType.DMA((flow_n + chem_n,)),
            pltpu.SemaphoreType.DMA((flow_n + chem_n,)),
        ],
        compiler_params=pltpu.CompilerParams(
            collective_id=0, has_side_effects=True, vmem_limit_bytes=VMEM_BYTES
        ),
        name="flux",
    )(levels, thermal_field, reciprocal_pair_diffusivity)

    advanced, heat = pl.pallas_call(
        burn_kernel,
        out_shape=(
            jax.ShapeDtypeStruct((species, rows, lanes), F32),
            jax.ShapeDtypeStruct((rows, lanes), F32),
        ),
        in_specs=[smem, anywhere, anywhere] + [vmem] * 7,
        out_specs=(anywhere, vmem),
        scratch_shapes=[
            pltpu.VMEM((rows, species, lanes), F32),
            pltpu.VMEM((rows, padded, lanes), F32),
            pltpu.VMEM((padded, GROUP * lanes), F32),
            pltpu.VMEM((reactions, GROUP * lanes), F32),
            pltpu.VMEM((reactions, GROUP * lanes), F32),
            pltpu.VMEM((reactions, depth), F32),
            pltpu.VMEM((depth, (reactions + 127) // 128 * 128), F32),
            pltpu.VMEM((padded, reactions), F32),
            pltpu.VMEM((reactions, 2 * depth), BF16),
            pltpu.VMEM((2 * padded, reactions), BF16),
            pltpu.SMEM((rows + GROUP,), jnp.int32),
            pltpu.SemaphoreType.DMA((rows,)),
            pltpu.SemaphoreType.DMA((chunks,)),
            pltpu.SemaphoreType.DMA(()),
        ],
        compiler_params=pltpu.CompilerParams(vmem_limit_bytes=VMEM_BYTES),
        name="burn",
    )(
        burning_flags.T, levels, flux, thermal_field, step, log_arrhenius_factor,
        kinetic_exponents, arrhenius_energies, molar_change_matrix, cooling_by_component[None],
    )
    return advanced.transpose(1, 0, 2), heat


def solution(mesh):
    placed = (
        P("flow", None, "chem"),
        P("flow", "chem"),
        P(),
        P(),
        P(),
        P(),
        P(),
        P(),
        P("flow", "chem"),
    )
    return jax.shard_map(
        partial(per_device, mesh.shape["flow"], mesh.shape["chem"]),
        mesh=mesh,
        in_specs=placed,
        out_specs=(P("flow", None, "chem"), P("flow", "chem")),
        check_vma=False,
    )
```

```python
from functools import partial
import math

import jax
import jax.numpy as jnp
from jax import lax
from jax.experimental import pallas as pl
from jax.experimental.pallas import tpu as pltpu
from jax.sharding import PartitionSpec as P

MESH = pl.DeviceIdType.MESH
F32 = jnp.float32
BF16 = jnp.bfloat16
courant = 0.2
chem_step = 0.05
log_offset = 0.001
rate_ceiling = 2.0
LOG2E = 1.0 / math.log(2.0)
CHUNK = 8
GROUP = 8
VMEM_BYTES = 56 * 2**20


def split(x):
    hi = x.astype(BF16)
    return hi, (x - hi.astype(F32)).astype(BF16)


def row_copies(start, k, species_hbm, rows_vmem, sem):
    for j in range(CHUNK):
        x = k * CHUNK + j
        copy = pltpu.make_async_copy(species_hbm.at[:, x], rows_vmem.at[x], sem.at[x])
        if start:
            copy.start()
        else:
            copy.wait()


def flux_kernel(
    flow_n, chem_n, c_hbm, t_ref, pair_ref, f_hbm, dt_ref,
    cv, cx, dx, fv, pairs, rr_ref, col_out, col_in, peak,
    in_sem, out_sem, halo_send, halo_recv, max_send, max_recv,
):
    rows, species, lanes = cv.shape
    padded = cx.shape[1]
    depth = pairs.shape[1]
    chunks = rows // CHUNK
    fi, ci = lax.axis_index("flow"), lax.axis_index("chem")

    def chunk_out(k):
        at = pl.ds(k * CHUNK, CHUNK)
        return pltpu.make_async_copy(fv.at[at], f_hbm.at[at], out_sem.at[k])

    @pl.loop(0, chunks)
    def _(k):
        row_copies(True, k, c_hbm, cv, in_sem)

    barrier = pltpu.get_barrier_semaphore()
    for k in range(1, flow_n):
        pl.semaphore_signal(barrier, inc=1, device_id=(lax.rem(fi + k, flow_n), ci), device_id_type=MESH)
    for k in range(1, chem_n):
        pl.semaphore_signal(barrier, inc=1, device_id=(fi, lax.rem(ci + k, chem_n)), device_id_type=MESH)

    at_col = lax.broadcasted_iota(jnp.int32, pairs.shape, 1)
    pairs[...] = jnp.where(at_col < species, 1.0, 0.0)
    pairs[0:species, 0:species] = pair_ref[...]
    hi, lo = split(pairs[...])
    rr_ref[...] = jnp.concatenate(
        [jnp.concatenate([hi, hi], axis=1), jnp.concatenate([lo, lo], axis=1)], axis=0
    )

    lane = lax.broadcasted_iota(jnp.int32, (padded, lanes), 1)

    def prepare(k, cols):
        row_copies(False, k, c_hbm, cv, in_sem)
        for j in range(CHUNK):
            x = k * CHUNK + j
            cx[x + 1, 0:species, :] = cv[x]
            cx[x + 1, species : species + 1, :] = t_ref[pl.ds(x, 1), :]
        cols = pltpu.roll(cols, lanes - 2 * CHUNK, 1)
        for j in range(CHUNK):
            at = lanes - 2 * CHUNK + 2 * j
            edges = pltpu.roll(cx[k * CHUNK + j + 1], at + 1, 1)
            cols = jnp.where((lane == at) | (lane == at + 1), edges, cols)
        return cols

    cols = lax.fori_loop(0, chunks, prepare, jnp.ones((padded, lanes), F32))
    cols = pltpu.roll(cols, 2 * rows, 1) if 2 * rows < lanes else cols
    col_out[0] = pltpu.roll(cols, lanes - 2, 1)
    col_out[1] = cols
    pl.semaphore_wait(barrier, flow_n + chem_n - 2)

    before, after = lax.rem(fi + flow_n - 1, flow_n), lax.rem(fi + 1, flow_n)
    west, east = lax.rem(ci + chem_n - 1, chem_n), lax.rem(ci + 1, chem_n)

    def halo(k, src, dst, device):
        return pltpu.make_async_remote_copy(
            src_ref=src, dst_ref=dst, send_sem=halo_send.at[k], recv_sem=halo_recv.at[k],
            device_id=device, device_id_type=MESH,
        )

    halos = [
        halo(0, cx.at[1], cx.at[rows + 1], (before, ci)),
        halo(1, cx.at[rows], cx.at[0], (after, ci)),
        halo(2, col_out.at[0], col_in.at[1], (fi, west)),
        halo(3, col_out.at[1], col_in.at[0], (fi, east)),
    ]
    for copy in halos:
        copy.start()

    def spreading(block):
        hi, lo = split(block)
        blank = jnp.zeros((depth - padded, block.shape[1]), BF16)
        total = jnp.dot(
            rr_ref[...], jnp.concatenate([hi, blank, lo, blank], axis=0), preferred_element_type=F32
        )
        heat = block[species : species + 1, :]
        return heat * jnp.sqrt(heat) / (total[:padded] + total[padded:])

    def diffusivities(k, top):
        first = k * CHUNK + 1
        d = spreading(jnp.concatenate([cx[first + j] for j in range(CHUNK)], axis=1))
        m = d[:, :lanes]
        for j in range(CHUNK):
            here = d[:, j * lanes : (j + 1) * lanes]
            dx[first + j] = here
            m = jnp.maximum(m, here)
        for s in range(0, padded, 8):
            top = jnp.maximum(top, m[s : s + 8])
        return top

    peak[0] = lax.fori_loop(0, chunks, diffusivities, jnp.zeros((8, lanes), F32))

    def spread_max(base, count, who):
        return [
            pltpu.make_async_remote_copy(
                src_ref=peak.at[base], dst_ref=peak.at[base + k],
                send_sem=max_send.at[base + k], recv_sem=max_recv.at[base + k],
                device_id=who(k), device_id_type=MESH,
            )
            for k in range(1, count)
        ]

    first = spread_max(0, flow_n, lambda k: (lax.rem(fi + k, flow_n), ci))
    for copy in first:
        copy.start()

    for copy in halos:
        copy.wait()
    zero = jnp.zeros((padded, lanes), F32)
    side = jnp.where(lax.rem(lane, 2) == 0, col_in[0], col_in[1])
    d = spreading(jnp.concatenate([cx[0], cx[rows + 1], side], axis=1))
    dx[0] = jnp.where(fi == 0, zero, d[:, :lanes])
    dx[rows + 1] = jnp.where(fi == flow_n - 1, zero, d[:, lanes : 2 * lanes])
    cx[0] = jnp.where(fi == 0, zero, cx[0])
    cx[rows + 1] = jnp.where(fi == flow_n - 1, zero, cx[rows + 1])
    outside = (lax.rem(lane, 2) == 0) & (ci == 0) | (lax.rem(lane, 2) == 1) & (ci == chem_n - 1)
    col_in[0] = jnp.where(outside, zero, side)
    col_in[1] = jnp.where(outside, zero, d[:, 2 * lanes :])

    half = padded // 2
    at_lane = lax.broadcasted_iota(jnp.int32, (half, lanes), 1)

    def flux_chunk(k):
        for j in range(CHUNK):
            x = k * CHUNK + j
            turn = (lanes - 2 * j) % lanes
            for s in range(0, padded, half):
                at = slice(s, s + half)
                c0, d0 = cx[x + 1, at, :], dx[x + 1, at, :]
                side_c, side_d = col_in[0, at, :], col_in[1, at, :]
                if turn:
                    side_c, side_d = pltpu.roll(side_c, turn, 1), pltpu.roll(side_d, turn, 1)
                left_c = jnp.where(at_lane == 0, side_c, pltpu.roll(c0, 1, 1))
                left_d = jnp.where(at_lane == 0, side_d, pltpu.roll(d0, 1, 1))
                left = (left_d + d0) * (c0 - left_c)
                total = (dx[x, at, :] + d0) * (cx[x, at, :] - c0)
                total = total + (dx[x + 2, at, :] + d0) * (cx[x + 2, at, :] - c0)
                right = jnp.where(
                    at_lane == lanes - 1, (side_d + d0) * (side_c - c0), pltpu.roll(left, lanes - 1, 1)
                )
                fv[x, at, :] = 0.5 * (total + (right - left))
        col_in[0] = pltpu.roll(col_in[0], lanes - 2 * CHUNK, 1)
        col_in[1] = pltpu.roll(col_in[1], lanes - 2 * CHUNK, 1)
        chunk_out(k).start()

    pl.loop(0, chunks // 2)(flux_chunk)

    for copy in first:
        copy.wait()
    top = peak[0]
    for k in range(1, flow_n):
        top = jnp.maximum(top, peak[k])
    peak[flow_n] = top
    second = spread_max(flow_n, chem_n, lambda k: (fi, lax.rem(ci + k, chem_n)))
    for copy in second:
        copy.start()
    pl.loop(chunks // 2, chunks)(flux_chunk)
    for copy in second:
        copy.wait()
    for k in range(1, chem_n):
        top = jnp.maximum(top, peak[flow_n + k])
    dt_ref[...] = courant / jnp.broadcast_to(
        jnp.max(jnp.max(top, axis=1, keepdims=True), axis=0, keepdims=True), dt_ref.shape
    )

    @pl.loop(0, chunks)
    def _(k):
        chunk_out(k).wait()


def burn_kernel(
    flag_ref, c_hbm, f_hbm, t_ref, dt_ref, factor_ref, order_ref, energy_ref, change_ref, cool_ref,
    o_hbm, to_ref,
    cv, fv, xs, base, rate, wide_k, side_k, wide_m, k_ref, m_ref, place, c_sem, f_sem, o_sem,
):
    rows, species, lanes = cv.shape
    padded = fv.shape[1]
    depth = wide_k.shape[1]
    reactions = wide_k.shape[0]
    chunks = rows // CHUNK
    width = GROUP * lanes

    def chunk_f(k):
        at = pl.ds(k * CHUNK, CHUNK)
        return pltpu.make_async_copy(f_hbm.at[at], fv.at[at], f_sem.at[k])

    def row_out(x):
        return pltpu.make_async_copy(cv.at[x], o_hbm.at[:, x], o_sem)

    @pl.loop(0, chunks)
    def _(k):
        row_copies(True, k, c_hbm, cv, c_sem)
        chunk_f(k).start()

    to_ref[...] = t_ref[...]

    def listed(x, count):
        place[count] = x
        return count + flag_ref[0, x]

    count = lax.fori_loop(0, rows, listed, jnp.int32(0))
    last = place[jnp.maximum(count - 1, 0)]
    for j in range(GROUP):
        place[count + j] = last

    wide_k[...] = jnp.zeros(wide_k.shape, F32)
    wide_k[:, 0:species] = order_ref[...]
    side_k[...] = jnp.zeros(side_k.shape, F32)
    side_k[species : species + 1, 0:reactions] = factor_ref[...].reshape(1, reactions)
    side_k[padded : padded + 1, 0:reactions] = -energy_ref[...].reshape(1, reactions)
    hi, lo = split((wide_k[...] + side_k[...].T[0:reactions, :]) * LOG2E)
    k_ref[:, 0:depth] = hi
    k_ref[:, depth:] = lo
    cooled = jnp.dot(
        jnp.broadcast_to(cool_ref[...], (8, species)), change_ref[...],
        precision=lax.Precision.HIGHEST, preferred_element_type=F32,
    )
    wide_m[...] = jnp.zeros(wide_m.shape, F32)
    wide_m[0:species, :] = change_ref[...]
    wide_m[species : species + 1, :] = -cooled[0:1]
    hi, lo = split(wide_m[...])
    m_ref[0:padded, :] = hi
    m_ref[padded:, :] = lo

    step = dt_ref[0:1, :]

    @pl.loop(0, chunks)
    def _(k):
        row_copies(False, k, c_hbm, cv, c_sem)
        chunk_f(k).wait()
        for j in range(CHUNK):
            x = k * CHUNK + j
            cv[x] = cv[x] + step * fv[x, 0:species, :]
        for j in range(CHUNK):
            x = k * CHUNK + j

            @pl.when(flag_ref[0, x] == 0)
            def _():
                row_out(x).start()

    row = lax.broadcasted_iota(jnp.int32, (padded, width), 0)
    extra = lax.broadcasted_iota(jnp.int32, (k_ref.shape[1] // 2 - padded, width), 0)
    ceiling = rate_ceiling * LOG2E

    @pl.loop(0, (count + GROUP - 1) // GROUP)
    def _(g):
        for j in range(GROUP):
            x = place[g * GROUP + j]
            at = slice(j * lanes, (j + 1) * lanes)
            xs[0:species, at] = cv[x]
            xs[species : species + 1, at] = t_ref[pl.ds(x, 1), :]
        x0 = xs[...]
        log1 = jnp.log(jnp.abs(x0) + log_offset)
        inverse = 1.0 / x0[species : species + 1, :]
        full = jnp.concatenate(
            [jnp.where(row == species, 1.0, log1), jnp.where(extra == 0, inverse, 0.0)], axis=0
        )
        hi, lo = split(full)
        terms = jnp.concatenate(
            [jnp.concatenate([hi, hi], axis=0), jnp.concatenate([lo, lo], axis=0)], axis=1
        )
        both = jnp.dot(k_ref[...], terms, preferred_element_type=F32)
        level = both[:, :width] + both[:, width:]
        base[...] = level
        r = jnp.exp2(jnp.minimum(level, ceiling))
        rate[...] = r
        hi, lo = split(r)
        wide = jnp.dot(m_ref[...], hi, preferred_element_type=F32)
        first = wide[:padded] + wide[padded:] + jnp.dot(m_ref[0:padded, :], lo, preferred_element_type=F32)

        def later(state):
            change = jnp.where(row == species, 0.0, jnp.log(jnp.abs(state) + log_offset) - log1)
            change = jnp.concatenate([change, jnp.zeros(extra.shape, F32)], axis=0).astype(BF16)
            level = base[...] + jnp.dot(
                k_ref[:, 0 : k_ref.shape[1] // 2], change, preferred_element_type=F32
            )
            r = jnp.exp2(jnp.minimum(level, ceiling))
            return first + jnp.dot(
                m_ref[0:padded, :], (r - rate[...]).astype(BF16), preferred_element_type=F32
            )

        second = later(x0 + (0.5 * chem_step) * first)
        total = first + 2.0 * second
        third = later(x0 + (0.5 * chem_step) * second)
        total = total + 2.0 * third
        total = total + later(x0 + chem_step * third)
        xs[...] = x0 + (chem_step / 6.0) * total
        for j in range(GROUP):
            x = place[g * GROUP + j]
            at = slice(j * lanes, (j + 1) * lanes)

            @pl.when(g * GROUP + j < count)
            def _():
                cv[x] = xs[0:species, at]
                to_ref[pl.ds(x, 1), :] = xs[species : species + 1, at]
                row_out(x).start()

    @pl.loop(0, rows)
    def _(x):
        row_out(x).wait()


def per_device(
    flow_n, chem_n,
    component_levels, thermal_field, reciprocal_pair_diffusivity, log_arrhenius_factor,
    kinetic_exponents, arrhenius_energies, molar_change_matrix, cooling_by_component, burning_flags,
):
    rows, species, lanes = component_levels.shape
    reactions = kinetic_exponents.shape[0]
    padded = (species + 16) // 16 * 16
    depth = (padded + 1 + 127) // 128 * 128
    chunks = rows // CHUNK

    levels = component_levels.transpose(1, 0, 2)
    vmem = pl.BlockSpec(memory_space=pltpu.VMEM)
    smem = pl.BlockSpec(memory_space=pltpu.SMEM)
    anywhere = pl.BlockSpec(memory_space=pl.ANY)
    flux, step = pl.pallas_call(
        partial(flux_kernel, flow_n, chem_n),
        out_shape=(
            jax.ShapeDtypeStruct((rows, padded, lanes), F32),
            jax.ShapeDtypeStruct((8, lanes), F32),
        ),
        in_specs=[anywhere, vmem, vmem],
        out_specs=(anywhere, vmem),
        scratch_shapes=[
            pltpu.VMEM((rows, species, lanes), F32),
            pltpu.VMEM((rows + 2, padded, lanes), F32),
            pltpu.VMEM((rows + 2, padded, lanes), F32),
            pltpu.VMEM((rows, padded, lanes), F32),
            pltpu.VMEM((padded, depth), F32),
            pltpu.VMEM((2 * padded, 2 * depth), BF16),
            pltpu.VMEM((2, padded, lanes), F32),
            pltpu.VMEM((2, padded, lanes), F32),
            pltpu.VMEM((flow_n + chem_n, 8, lanes), F32),
            pltpu.SemaphoreType.DMA((rows,)),
            pltpu.SemaphoreType.DMA((chunks,)),
            pltpu.SemaphoreType.DMA((4,)),
            pltpu.SemaphoreType.DMA((4,)),
            pltpu.SemaphoreType.DMA((flow_n + chem_n,)),
            pltpu.SemaphoreType.DMA((flow_n + chem_n,)),
        ],
        compiler_params=pltpu.CompilerParams(
            collective_id=0, has_side_effects=True, vmem_limit_bytes=VMEM_BYTES
        ),
        name="flux",
    )(levels, thermal_field, reciprocal_pair_diffusivity)

    advanced, heat = pl.pallas_call(
        burn_kernel,
        out_shape=(
            jax.ShapeDtypeStruct((species, rows, lanes), F32),
            jax.ShapeDtypeStruct((rows, lanes), F32),
        ),
        in_specs=[smem, anywhere, anywhere] + [vmem] * 7,
        out_specs=(anywhere, vmem),
        scratch_shapes=[
            pltpu.VMEM((rows, species, lanes), F32),
            pltpu.VMEM((rows, padded, lanes), F32),
            pltpu.VMEM((padded, GROUP * lanes), F32),
            pltpu.VMEM((reactions, GROUP * lanes), F32),
            pltpu.VMEM((reactions, GROUP * lanes), F32),
            pltpu.VMEM((reactions, depth), F32),
            pltpu.VMEM((depth, (reactions + 127) // 128 * 128), F32),
            pltpu.VMEM((padded, reactions), F32),
            pltpu.VMEM((reactions, 2 * depth), BF16),
            pltpu.VMEM((2 * padded, reactions), BF16),
            pltpu.SMEM((rows + GROUP,), jnp.int32),
            pltpu.SemaphoreType.DMA((rows,)),
            pltpu.SemaphoreType.DMA((chunks,)),
            pltpu.SemaphoreType.DMA(()),
        ],
        compiler_params=pltpu.CompilerParams(vmem_limit_bytes=VMEM_BYTES),
        name="burn",
    )(
        burning_flags.T, levels, flux, thermal_field, step, log_arrhenius_factor,
        kinetic_exponents, arrhenius_energies, molar_change_matrix, cooling_by_component[None],
    )
    return advanced.transpose(1, 0, 2), heat


def solution(mesh):
    placed = (
        P("flow", None, "chem"),
        P("flow", "chem"),
        P(),
        P(),
        P(),
        P(),
        P(),
        P(),
        P("flow", "chem"),
    )
    return jax.shard_map(
        partial(per_device, mesh.shape["flow"], mesh.shape["chem"]),
        mesh=mesh,
        in_specs=placed,
        out_specs=(P("flow", None, "chem"), P("flow", "chem")),
        check_vma=False,
    )
```

```python
from functools import partial
import math

import jax
import jax.numpy as jnp
from jax import lax
from jax.experimental import pallas as pl
from jax.experimental.pallas import tpu as pltpu
from jax.sharding import PartitionSpec as P

MESH = pl.DeviceIdType.MESH
F32 = jnp.float32
BF16 = jnp.bfloat16
courant = 0.2
chem_step = 0.05
log_offset = 0.001
rate_ceiling = 2.0
LOG2E = 1.0 / math.log(2.0)
CHUNK = 8
GROUP = 8
SLABS = 6
VMEM_BYTES = 56 * 2**20


def split(x):
    hi = x.astype(BF16)
    return hi, (x - hi.astype(F32)).astype(BF16)


def row_copies(start, k, species_hbm, rows_vmem, sem):
    for j in range(CHUNK):
        x = k * CHUNK + j
        copy = pltpu.make_async_copy(species_hbm.at[:, x], rows_vmem.at[x], sem.at[x])
        if start:
            copy.start()
        else:
            copy.wait()


def flux_kernel(
    flow_n, chem_n, c_hbm, t_ref, pair_ref, f_hbm, dt_ref,
    cv, cx, dx, fv, pairs, rr_ref, col_out, col_in, peak,
    in_sem, out_sem, halo_send, halo_recv, max_send, max_recv,
):
    rows, species, lanes = cv.shape
    padded = cx.shape[1]
    depth = pairs.shape[1]
    chunks = rows // CHUNK
    fi, ci = lax.axis_index("flow"), lax.axis_index("chem")

    def row_out(x):
        return pltpu.make_async_copy(fv.at[x], f_hbm.at[:, x], out_sem.at[x])

    @pl.loop(0, chunks)
    def _(k):
        row_copies(True, k, c_hbm, cv, in_sem)

    barrier = pltpu.get_barrier_semaphore()
    for k in range(1, flow_n):
        pl.semaphore_signal(barrier, inc=1, device_id=(lax.rem(fi + k, flow_n), ci), device_id_type=MESH)
    for k in range(1, chem_n):
        pl.semaphore_signal(barrier, inc=1, device_id=(fi, lax.rem(ci + k, chem_n)), device_id_type=MESH)

    at_col = lax.broadcasted_iota(jnp.int32, pairs.shape, 1)
    pairs[...] = jnp.where(at_col < species, 1.0, 0.0)
    pairs[0:species, 0:species] = pair_ref[...]
    hi, lo = split(pairs[...])
    rr_ref[...] = jnp.concatenate(
        [jnp.concatenate([hi, hi], axis=1), jnp.concatenate([lo, lo], axis=1)], axis=0
    )

    lane = lax.broadcasted_iota(jnp.int32, (padded, lanes), 1)

    def prepare(k, cols):
        row_copies(False, k, c_hbm, cv, in_sem)
        for j in range(CHUNK):
            x = k * CHUNK + j
            cx[x + 1, 0:species, :] = cv[x]
            cx[x + 1, species : species + 1, :] = t_ref[pl.ds(x, 1), :]
        cols = pltpu.roll(cols, lanes - 2 * CHUNK, 1)
        for j in range(CHUNK):
            at = lanes - 2 * CHUNK + 2 * j
            edges = pltpu.roll(cx[k * CHUNK + j + 1], at + 1, 1)
            cols = jnp.where((lane == at) | (lane == at + 1), edges, cols)
        return cols

    cols = lax.fori_loop(0, chunks, prepare, jnp.ones((padded, lanes), F32))
    cols = pltpu.roll(cols, 2 * rows, 1) if 2 * rows < lanes else cols
    col_out[0] = pltpu.roll(cols, lanes - 2, 1)
    col_out[1] = cols
    pl.semaphore_wait(barrier, flow_n + chem_n - 2)

    before, after = lax.rem(fi + flow_n - 1, flow_n), lax.rem(fi + 1, flow_n)
    west, east = lax.rem(ci + chem_n - 1, chem_n), lax.rem(ci + 1, chem_n)

    def halo(k, src, dst, device):
        return pltpu.make_async_remote_copy(
            src_ref=src, dst_ref=dst, send_sem=halo_send.at[k], recv_sem=halo_recv.at[k],
            device_id=device, device_id_type=MESH,
        )

    halos = [
        halo(0, cx.at[1], cx.at[rows + 1], (before, ci)),
        halo(1, cx.at[rows], cx.at[0], (after, ci)),
        halo(2, col_out.at[0], col_in.at[1], (fi, west)),
        halo(3, col_out.at[1], col_in.at[0], (fi, east)),
    ]
    for copy in halos:
        copy.start()

    def spreading(block):
        hi, lo = split(block)
        blank = jnp.zeros((depth - padded, block.shape[1]), BF16)
        total = jnp.dot(
            rr_ref[...], jnp.concatenate([hi, blank, lo, blank], axis=0), preferred_element_type=F32
        )
        heat = block[species : species + 1, :]
        total = total[:padded] + total[padded:]
        guess = pl.reciprocal(total, approx=True)
        guess = guess * (2.0 - total * guess)
        return heat * jnp.sqrt(heat) * (guess * (2.0 - total * guess))

    def diffusivities(k, top):
        first = k * CHUNK + 1
        d = spreading(jnp.concatenate([cx[first + j] for j in range(CHUNK)], axis=1))
        m = d[:, :lanes]
        for j in range(CHUNK):
            here = d[:, j * lanes : (j + 1) * lanes]
            dx[first + j] = here
            m = jnp.maximum(m, here)
        for s in range(0, padded, 8):
            top = jnp.maximum(top, m[s : s + 8])
        return top

    peak[0] = lax.fori_loop(0, chunks, diffusivities, jnp.zeros((8, lanes), F32))

    def spread_max(base, count, who):
        return [
            pltpu.make_async_remote_copy(
                src_ref=peak.at[base], dst_ref=peak.at[base + k],
                send_sem=max_send.at[base + k], recv_sem=max_recv.at[base + k],
                device_id=who(k), device_id_type=MESH,
            )
            for k in range(1, count)
        ]

    first = spread_max(0, flow_n, lambda k: (lax.rem(fi + k, flow_n), ci))
    for copy in first:
        copy.start()

    for copy in halos:
        copy.wait()
    zero = jnp.zeros((padded, lanes), F32)
    side = jnp.where(lax.rem(lane, 2) == 0, col_in[0], col_in[1])
    own = pltpu.roll(col_out[1], lanes - 1, 1)
    d = spreading(jnp.concatenate([cx[0], cx[rows + 1], side, own], axis=1))
    dx[0] = jnp.where(fi == 0, zero, d[:, :lanes])
    dx[rows + 1] = jnp.where(fi == flow_n - 1, zero, d[:, lanes : 2 * lanes])
    cx[0] = jnp.where(fi == 0, zero, cx[0])
    cx[rows + 1] = jnp.where(fi == flow_n - 1, zero, cx[rows + 1])
    outside = (lax.rem(lane, 2) == 0) & (ci == 0) | (lax.rem(lane, 2) == 1) & (ci == chem_n - 1)
    side_c = jnp.where(outside, zero, side)
    side_d = jnp.where(outside, zero, d[:, 2 * lanes : 3 * lanes])
    edge = (side_d + d[:, 3 * lanes :]) * (own - side_c)
    col_in[0] = jnp.where(lax.rem(lane, 2) == 0, edge, -edge)

    half = padded // 2
    at_lanes = lax.broadcasted_iota(jnp.int32, (half, lanes), 1)

    def flux_chunk(k):
        for j in range(CHUNK):
            x = k * CHUNK + j
            turn = (lanes - 2 * j) % lanes
            for s in range(0, padded, half):
                at = slice(s, min(s + half, species))
                at_lane = at_lanes[: at.stop - s]
                c0, d0 = cx[x + 1, at, :], dx[x + 1, at, :]
                edge = col_in[0, at, :]
                if turn:
                    edge = pltpu.roll(edge, turn, 1)
                left = (pltpu.roll(d0, 1, 1) + d0) * (c0 - pltpu.roll(c0, 1, 1))
                left = jnp.where(at_lane == 0, edge, left)
                total = (dx[x, at, :] + d0) * (cx[x, at, :] - c0)
                total = total + (dx[x + 2, at, :] + d0) * (cx[x + 2, at, :] - c0)
                right = jnp.where(at_lane == lanes - 1, edge, pltpu.roll(left, lanes - 1, 1))
                fv[x, at, :] = 0.5 * (total + (right - left))
        col_in[0] = pltpu.roll(col_in[0], lanes - 2 * CHUNK, 1)
        for j in range(CHUNK):
            row_out(k * CHUNK + j).start()

    pl.loop(0, chunks // 2)(flux_chunk)

    for copy in first:
        copy.wait()
    top = peak[0]
    for k in range(1, flow_n):
        top = jnp.maximum(top, peak[k])
    peak[flow_n] = top
    second = spread_max(flow_n, chem_n, lambda k: (fi, lax.rem(ci + k, chem_n)))
    for copy in second:
        copy.start()
    pl.loop(chunks // 2, chunks)(flux_chunk)
    for copy in second:
        copy.wait()
    for k in range(1, chem_n):
        top = jnp.maximum(top, peak[flow_n + k])
    dt_ref[...] = courant / jnp.broadcast_to(
        jnp.max(jnp.max(top, axis=1, keepdims=True), axis=0, keepdims=True), dt_ref.shape
    )

    @pl.loop(0, chunks)
    def _(k):
        for j in range(CHUNK):
            row_out(k * CHUNK + j).wait()


def burn_kernel(
    flag_ref, c_hbm, f_hbm, t_ref, dt_ref, factor_ref, order_ref, energy_ref, change_ref, cool_ref,
    o_hbm, to_ref,
    cv, fv, cg, fg, xs, base, rate, wide_k, side_k, wide_m, k_ref, m_ref, place,
    c_sem, f_sem, o_sem, cg_sem, fg_sem, row_sem,
):
    species, rows, lanes = cv.shape
    padded = wide_m.shape[0]
    depth = wide_k.shape[1]
    reactions = wide_k.shape[0]
    slabs = c_sem.shape[0]
    slab = -(-species // slabs)
    width = GROUP * lanes

    def part(k, source, target, sems):
        at = slice(k * slab, min((k + 1) * slab, species))
        return pltpu.make_async_copy(source.at[at], target.at[at], sems.at[k])

    def gather(s, source, target, sem):
        return pltpu.make_async_copy(source.at[:, place[s]], target.at[s], sem)

    def row_out(s):
        return pltpu.make_async_copy(cg.at[s], o_hbm.at[:, place[s]], row_sem)

    to_ref[...] = t_ref[...]

    def listed(x, count):
        place[count] = x
        return count + flag_ref[0, x]

    count = lax.fori_loop(0, rows, listed, jnp.int32(0))
    groups = (count + GROUP - 1) // GROUP
    last = place[jnp.maximum(count - 1, 0)]
    for j in range(GROUP):
        place[count + j] = last

    @pl.loop(0, groups * GROUP)
    def _(s):
        gather(s, c_hbm, cg, cg_sem).start()
        gather(s, f_hbm, fg, fg_sem).start()

    for k in range(slabs):
        part(k, c_hbm, cv, c_sem).start()
        part(k, f_hbm, fv, f_sem).start()

    wide_k[...] = jnp.zeros(wide_k.shape, F32)
    wide_k[:, 0:species] = order_ref[...]
    side_k[...] = jnp.zeros(side_k.shape, F32)
    side_k[species : species + 1, 0:reactions] = factor_ref[...].reshape(1, reactions)
    side_k[padded : padded + 1, 0:reactions] = -energy_ref[...].reshape(1, reactions)
    hi, lo = split((wide_k[...] + side_k[...].T[0:reactions, :]) * LOG2E)
    k_ref[:, 0:depth] = hi
    k_ref[:, depth:] = lo
    cooled = jnp.dot(
        jnp.broadcast_to(cool_ref[...], (8, species)), change_ref[...],
        precision=lax.Precision.HIGHEST, preferred_element_type=F32,
    )
    wide_m[...] = jnp.zeros(wide_m.shape, F32)
    wide_m[0:species, :] = change_ref[...]
    wide_m[species : species + 1, :] = -cooled[0:1]
    hi, lo = split(wide_m[...])
    m_ref[0:padded, :] = hi
    m_ref[padded:, :] = lo

    step = dt_ref[0:1, :]

    for k in range(slabs):
        part(k, c_hbm, cv, c_sem).wait()
        part(k, f_hbm, fv, f_sem).wait()
        first, final = k * slab, min((k + 1) * slab, species)
        for i in range(first, final):
            cv[i] = cv[i] + step * fv[i]
        part(k, cv, o_hbm, o_sem).start()

    @pl.loop(0, groups * GROUP)
    def _(s):
        gather(s, c_hbm, cg, cg_sem).wait()
        gather(s, f_hbm, fg, fg_sem).wait()

    row = lax.broadcasted_iota(jnp.int32, (padded, width), 0)
    extra = lax.broadcasted_iota(jnp.int32, (k_ref.shape[1] // 2 - padded, width), 0)
    ceiling = rate_ceiling * LOG2E

    @pl.loop(0, groups)
    def _(g):
        for j in range(GROUP):
            x = place[g * GROUP + j]
            at = slice(j * lanes, (j + 1) * lanes)
            s = g * GROUP + j
            xs[0:species, at] = cg[s] + step * fg[s]
            xs[species : species + 1, at] = t_ref[pl.ds(x, 1), :]
        x0 = xs[...]
        log1 = jnp.log(jnp.abs(x0) + log_offset)
        inverse = 1.0 / x0[species : species + 1, :]
        full = jnp.concatenate(
            [jnp.where(row == species, 1.0, log1), jnp.where(extra == 0, inverse, 0.0)], axis=0
        )
        hi, lo = split(full)
        terms = jnp.concatenate(
            [jnp.concatenate([hi, hi], axis=0), jnp.concatenate([lo, lo], axis=0)], axis=1
        )
        both = jnp.dot(k_ref[...], terms, preferred_element_type=F32)
        level = both[:, :width] + both[:, width:]
        base[...] = level
        r = jnp.exp2(jnp.minimum(level, ceiling))
        rate[...] = r
        hi, lo = split(r)
        wide = jnp.dot(m_ref[...], hi, preferred_element_type=F32)
        first = wide[:padded] + wide[padded:] + jnp.dot(m_ref[0:padded, :], lo, preferred_element_type=F32)

        def later(state):
            change = jnp.where(row == species, 0.0, jnp.log(jnp.abs(state) + log_offset) - log1)
            change = jnp.concatenate([change, jnp.zeros(extra.shape, F32)], axis=0).astype(BF16)
            level = base[...] + jnp.dot(
                k_ref[:, 0 : k_ref.shape[1] // 2], change, preferred_element_type=F32
            )
            r = jnp.exp2(jnp.minimum(level, ceiling))
            return first + jnp.dot(
                m_ref[0:padded, :], (r - rate[...]).astype(BF16), preferred_element_type=F32
            )

        second = later(x0 + (0.5 * chem_step) * first)
        total = first + 2.0 * second
        third = later(x0 + (0.5 * chem_step) * second)
        total = total + 2.0 * third
        total = total + later(x0 + chem_step * third)
        xs[...] = x0 + (chem_step / 6.0) * total
        @pl.when(g == 0)
        def _():
            for k in range(slabs):
                part(k, cv, o_hbm, o_sem).wait()

        for j in range(GROUP):
            s = g * GROUP + j
            at = slice(j * lanes, (j + 1) * lanes)

            @pl.when(s < count)
            def _():
                cg[s] = xs[0:species, at]
                to_ref[pl.ds(place[s], 1), :] = xs[species : species + 1, at]
                row_out(s).start()

    @pl.when(groups == 0)
    def _():
        for k in range(slabs):
            part(k, cv, o_hbm, o_sem).wait()

    @pl.loop(0, count)
    def _(s):
        row_out(s).wait()


def per_device(
    flow_n, chem_n,
    component_levels, thermal_field, reciprocal_pair_diffusivity, log_arrhenius_factor,
    kinetic_exponents, arrhenius_energies, molar_change_matrix, cooling_by_component, burning_flags,
):
    rows, species, lanes = component_levels.shape
    reactions = kinetic_exponents.shape[0]
    padded = (species + 16) // 16 * 16
    depth = (padded + 1 + 127) // 128 * 128
    chunks = rows // CHUNK
    most = (3 * rows // 8 + GROUP - 1) // GROUP * GROUP

    levels = component_levels.transpose(1, 0, 2)
    vmem = pl.BlockSpec(memory_space=pltpu.VMEM)
    smem = pl.BlockSpec(memory_space=pltpu.SMEM)
    anywhere = pl.BlockSpec(memory_space=pl.ANY)
    flux, step = pl.pallas_call(
        partial(flux_kernel, flow_n, chem_n),
        out_shape=(
            jax.ShapeDtypeStruct((species, rows, lanes), F32),
            jax.ShapeDtypeStruct((8, lanes), F32),
        ),
        in_specs=[anywhere, vmem, vmem],
        out_specs=(anywhere, vmem),
        scratch_shapes=[
            pltpu.VMEM((rows, species, lanes), F32),
            pltpu.VMEM((rows + 2, padded, lanes), F32),
            pltpu.VMEM((rows + 2, padded, lanes), F32),
            pltpu.VMEM((rows, species, lanes), F32),
            pltpu.VMEM((padded, depth), F32),
            pltpu.VMEM((2 * padded, 2 * depth), BF16),
            pltpu.VMEM((2, padded, lanes), F32),
            pltpu.VMEM((2, padded, lanes), F32),
            pltpu.VMEM((flow_n + chem_n, 8, lanes), F32),
            pltpu.SemaphoreType.DMA((rows,)),
            pltpu.SemaphoreType.DMA((rows,)),
            pltpu.SemaphoreType.DMA((4,)),
            pltpu.SemaphoreType.DMA((4,)),
            pltpu.SemaphoreType.DMA((flow_n + chem_n,)),
            pltpu.SemaphoreType.DMA((flow_n + chem_n,)),
        ],
        compiler_params=pltpu.CompilerParams(
            collective_id=0, has_side_effects=True, vmem_limit_bytes=VMEM_BYTES
        ),
        name="flux",
    )(levels, thermal_field, reciprocal_pair_diffusivity)

    advanced, heat = pl.pallas_call(
        burn_kernel,
        out_shape=(
            jax.ShapeDtypeStruct((species, rows, lanes), F32),
            jax.ShapeDtypeStruct((rows, lanes), F32),
        ),
        in_specs=[smem, anywhere, anywhere] + [vmem] * 7,
        out_specs=(anywhere, vmem),
        scratch_shapes=[
            pltpu.VMEM((species, rows, lanes), F32),
            pltpu.VMEM((species, rows, lanes), F32),
            pltpu.VMEM((most, species, lanes), F32),
            pltpu.VMEM((most, species, lanes), F32),
            pltpu.VMEM((padded, GROUP * lanes), F32),
            pltpu.VMEM((reactions, GROUP * lanes), F32),
            pltpu.VMEM((reactions, GROUP * lanes), F32),
            pltpu.VMEM((reactions, depth), F32),
            pltpu.VMEM((depth, (reactions + 127) // 128 * 128), F32),
            pltpu.VMEM((padded, reactions), F32),
            pltpu.VMEM((reactions, 2 * depth), BF16),
            pltpu.VMEM((2 * padded, reactions), BF16),
            pltpu.SMEM((rows + GROUP,), jnp.int32),
            pltpu.SemaphoreType.DMA((SLABS,)),
            pltpu.SemaphoreType.DMA((SLABS,)),
            pltpu.SemaphoreType.DMA((SLABS,)),
            pltpu.SemaphoreType.DMA(()),
            pltpu.SemaphoreType.DMA(()),
            pltpu.SemaphoreType.DMA(()),
        ],
        compiler_params=pltpu.CompilerParams(vmem_limit_bytes=VMEM_BYTES),
        name="burn",
    )(
        burning_flags.T, levels, flux, thermal_field, step, log_arrhenius_factor,
        kinetic_exponents, arrhenius_energies, molar_change_matrix, cooling_by_component[None],
    )
    return advanced.transpose(1, 0, 2), heat


def solution(mesh):
    placed = (
        P("flow", None, "chem"),
        P("flow", "chem"),
        P(),
        P(),
        P(),
        P(),
        P(),
        P(),
        P("flow", "chem"),
    )
    return jax.shard_map(
        partial(per_device, mesh.shape["flow"], mesh.shape["chem"]),
        mesh=mesh,
        in_specs=placed,
        out_specs=(P("flow", None, "chem"), P("flow", "chem")),
        check_vma=False,
    )
```

```python
from functools import partial
import math

import jax
import jax.numpy as jnp
from jax import lax
from jax.experimental import pallas as pl
from jax.experimental.pallas import tpu as pltpu
from jax.sharding import PartitionSpec as P

MESH = pl.DeviceIdType.MESH
F32 = jnp.float32
BF16 = jnp.bfloat16
courant = 0.2
chem_step = 0.05
log_offset = 0.001
rate_ceiling = 2.0
LOG2E = 1.0 / math.log(2.0)
CHUNK = 8
GROUP = 8
WIDE = 4
VMEM_BYTES = 56 * 2**20


def split(x):
    hi = x.astype(BF16)
    return hi, (x - hi.astype(F32)).astype(BF16)


def row_copies(start, k, species_hbm, rows_vmem, sem):
    for j in range(CHUNK):
        x = k * CHUNK + j
        copy = pltpu.make_async_copy(species_hbm.at[:, x], rows_vmem.at[x], sem.at[x])
        if start:
            copy.start()
        else:
            copy.wait()


def flux_kernel(
    flow_n, chem_n, c_hbm, t_ref, pair_ref, f_hbm, dt_ref,
    cv, cx, dx, fv, pairs, rr_ref, col_out, col_in, peak,
    in_sem, out_sem, halo_send, halo_recv, max_send, max_recv,
):
    rows, species, lanes = cv.shape
    padded = cx.shape[1]
    depth = pairs.shape[1]
    chunks = rows // CHUNK
    fi, ci = lax.axis_index("flow"), lax.axis_index("chem")

    def chunk_out(k):
        at = pl.ds(k * CHUNK, CHUNK)
        return pltpu.make_async_copy(fv.at[at], f_hbm.at[at], out_sem.at[k])

    @pl.loop(0, chunks)
    def _(k):
        row_copies(True, k, c_hbm, cv, in_sem)

    barrier = pltpu.get_barrier_semaphore()
    for k in range(1, flow_n):
        pl.semaphore_signal(barrier, inc=1, device_id=(lax.rem(fi + k, flow_n), ci), device_id_type=MESH)
    for k in range(1, chem_n):
        pl.semaphore_signal(barrier, inc=1, device_id=(fi, lax.rem(ci + k, chem_n)), device_id_type=MESH)

    at_col = lax.broadcasted_iota(jnp.int32, pairs.shape, 1)
    pairs[...] = jnp.where(at_col < species, 1.0, 0.0)
    pairs[0:species, 0:species] = pair_ref[...]
    hi, lo = split(pairs[...])
    rr_ref[...] = jnp.concatenate(
        [jnp.concatenate([hi, hi], axis=1), jnp.concatenate([lo, lo], axis=1)], axis=0
    )

    lane = lax.broadcasted_iota(jnp.int32, (padded, lanes), 1)

    def prepare(k, cols):
        row_copies(False, k, c_hbm, cv, in_sem)
        for j in range(CHUNK):
            x = k * CHUNK + j
            cx[x + 1, 0:species, :] = cv[x]
            cx[x + 1, species : species + 1, :] = t_ref[pl.ds(x, 1), :]
        cols = pltpu.roll(cols, lanes - 2 * CHUNK, 1)
        for j in range(CHUNK):
            at = lanes - 2 * CHUNK + 2 * j
            edges = pltpu.roll(cx[k * CHUNK + j + 1], at + 1, 1)
            cols = jnp.where((lane == at) | (lane == at + 1), edges, cols)
        return cols

    cols = lax.fori_loop(0, chunks, prepare, jnp.ones((padded, lanes), F32))
    cols = pltpu.roll(cols, 2 * rows, 1) if 2 * rows < lanes else cols
    col_out[0] = pltpu.roll(cols, lanes - 2, 1)
    col_out[1] = cols
    pl.semaphore_wait(barrier, flow_n + chem_n - 2)

    before, after = lax.rem(fi + flow_n - 1, flow_n), lax.rem(fi + 1, flow_n)
    west, east = lax.rem(ci + chem_n - 1, chem_n), lax.rem(ci + 1, chem_n)

    def halo(k, src, dst, device):
        return pltpu.make_async_remote_copy(
            src_ref=src, dst_ref=dst, send_sem=halo_send.at[k], recv_sem=halo_recv.at[k],
            device_id=device, device_id_type=MESH,
        )

    halos = [
        halo(0, cx.at[1], cx.at[rows + 1], (before, ci)),
        halo(1, cx.at[rows], cx.at[0], (after, ci)),
        halo(2, col_out.at[0], col_in.at[1], (fi, west)),
        halo(3, col_out.at[1], col_in.at[0], (fi, east)),
    ]
    for copy in halos:
        copy.start()

    def spreading(block):
        hi, lo = split(block)
        blank = jnp.zeros((depth - padded, block.shape[1]), BF16)
        total = jnp.dot(
            rr_ref[...], jnp.concatenate([hi, blank, lo, blank], axis=0), preferred_element_type=F32
        )
        heat = block[species : species + 1, :]
        total = total[:padded] + total[padded:]
        guess = pl.reciprocal(total, approx=True)
        guess = guess * (2.0 - total * guess)
        return heat * jnp.sqrt(heat) * (guess * (2.0 - total * guess))

    def diffusivities(k, top):
        first = k * CHUNK + 1
        d = spreading(jnp.concatenate([cx[first + j] for j in range(CHUNK)], axis=1))
        m = d[:, :lanes]
        for j in range(CHUNK):
            here = d[:, j * lanes : (j + 1) * lanes]
            dx[first + j] = here
            m = jnp.maximum(m, here)
        for s in range(0, padded, 8):
            top = jnp.maximum(top, m[s : s + 8])
        return top

    peak[0] = lax.fori_loop(0, chunks, diffusivities, jnp.zeros((8, lanes), F32))

    def spread_max(base, count, who):
        return [
            pltpu.make_async_remote_copy(
                src_ref=peak.at[base], dst_ref=peak.at[base + k],
                send_sem=max_send.at[base + k], recv_sem=max_recv.at[base + k],
                device_id=who(k), device_id_type=MESH,
            )
            for k in range(1, count)
        ]

    first = spread_max(0, flow_n, lambda k: (lax.rem(fi + k, flow_n), ci))
    for copy in first:
        copy.start()

    for copy in halos:
        copy.wait()
    zero = jnp.zeros((padded, lanes), F32)
    side = jnp.where(lax.rem(lane, 2) == 0, col_in[0], col_in[1])
    own = pltpu.roll(col_out[1], lanes - 1, 1)
    d = spreading(jnp.concatenate([cx[0], cx[rows + 1], side, own], axis=1))
    dx[0] = jnp.where(fi == 0, zero, d[:, :lanes])
    dx[rows + 1] = jnp.where(fi == flow_n - 1, zero, d[:, lanes : 2 * lanes])
    cx[0] = jnp.where(fi == 0, zero, cx[0])
    cx[rows + 1] = jnp.where(fi == flow_n - 1, zero, cx[rows + 1])
    outside = (lax.rem(lane, 2) == 0) & (ci == 0) | (lax.rem(lane, 2) == 1) & (ci == chem_n - 1)
    side_c = jnp.where(outside, zero, side)
    side_d = jnp.where(outside, zero, d[:, 2 * lanes : 3 * lanes])
    edge = (side_d + d[:, 3 * lanes :]) * (own - side_c)
    col_in[0] = jnp.where(lax.rem(lane, 2) == 0, edge, -edge)

    wide = (WIDE, padded, lanes)
    at_lane = lax.broadcasted_iota(jnp.int32, wide, 2)

    def flux_chunk(k):
        edges = col_in[0]
        for j in range(0, CHUNK, WIDE):
            x = k * CHUNK + j
            c, d = cx[pl.ds(x, WIDE + 2)], dx[pl.ds(x, WIDE + 2)]
            c0, d0 = c[1:-1], d[1:-1]
            edge = jnp.stack(
                [
                    pltpu.roll(edges, lanes - 2 * (j + i), 1) if j + i else edges
                    for i in range(WIDE)
                ]
            )
            left = (pltpu.roll(d0, 1, 2) + d0) * (c0 - pltpu.roll(c0, 1, 2))
            left = jnp.where(at_lane == 0, edge, left)
            right = jnp.where(at_lane == lanes - 1, edge, pltpu.roll(left, lanes - 1, 2))
            face = (d[1:] + d[:-1]) * (c[1:] - c[:-1])
            fv[pl.ds(x, WIDE)] = 0.5 * ((face[1:] - face[:-1]) + (right - left))
        col_in[0] = pltpu.roll(edges, lanes - 2 * CHUNK, 1)
        chunk_out(k).start()

    pl.loop(0, chunks // 2)(flux_chunk)

    for copy in first:
        copy.wait()
    top = peak[0]
    for k in range(1, flow_n):
        top = jnp.maximum(top, peak[k])
    peak[flow_n] = top
    second = spread_max(flow_n, chem_n, lambda k: (fi, lax.rem(ci + k, chem_n)))
    for copy in second:
        copy.start()
    pl.loop(chunks // 2, chunks)(flux_chunk)
    for copy in second:
        copy.wait()
    for k in range(1, chem_n):
        top = jnp.maximum(top, peak[flow_n + k])
    dt_ref[...] = courant / jnp.broadcast_to(
        jnp.max(jnp.max(top, axis=1, keepdims=True), axis=0, keepdims=True), dt_ref.shape
    )

    @pl.loop(0, chunks)
    def _(k):
        chunk_out(k).wait()


def burn_kernel(
    flag_ref, c_hbm, f_hbm, t_ref, dt_ref, factor_ref, order_ref, energy_ref, change_ref, cool_ref,
    o_hbm, to_ref,
    cv, fv, xs, base, rate, wide_k, side_k, wide_m, k_ref, m_ref, place, c_sem, f_sem, o_sem,
):
    rows, species, lanes = cv.shape
    padded = fv.shape[1]
    depth = wide_k.shape[1]
    reactions = wide_k.shape[0]
    chunks = rows // CHUNK
    width = GROUP * lanes

    def chunk_f(k):
        at = pl.ds(k * CHUNK, CHUNK)
        return pltpu.make_async_copy(f_hbm.at[at], fv.at[at], f_sem.at[k])

    def row_out(x):
        return pltpu.make_async_copy(cv.at[x], o_hbm.at[:, x], o_sem)

    @pl.loop(0, chunks)
    def _(k):
        row_copies(True, k, c_hbm, cv, c_sem)
        chunk_f(k).start()

    to_ref[...] = t_ref[...]

    def listed(x, count):
        place[count] = x
        return count + flag_ref[0, x]

    count = lax.fori_loop(0, rows, listed, jnp.int32(0))
    last = place[jnp.maximum(count - 1, 0)]
    for j in range(GROUP):
        place[count + j] = last

    wide_k[...] = jnp.zeros(wide_k.shape, F32)
    wide_k[:, 0:species] = order_ref[...]
    side_k[...] = jnp.zeros(side_k.shape, F32)
    side_k[species : species + 1, 0:reactions] = factor_ref[...].reshape(1, reactions)
    side_k[padded : padded + 1, 0:reactions] = -energy_ref[...].reshape(1, reactions)
    hi, lo = split((wide_k[...] + side_k[...].T[0:reactions, :]) * LOG2E)
    k_ref[:, 0:depth] = hi
    k_ref[:, depth:] = lo
    cooled = jnp.dot(
        jnp.broadcast_to(cool_ref[...], (8, species)), change_ref[...],
        precision=lax.Precision.HIGHEST, preferred_element_type=F32,
    )
    wide_m[...] = jnp.zeros(wide_m.shape, F32)
    wide_m[0:species, :] = change_ref[...]
    wide_m[species : species + 1, :] = -cooled[0:1]
    hi, lo = split(wide_m[...])
    m_ref[0:padded, :] = hi
    m_ref[padded:, :] = lo

    step = dt_ref[0:1, :]

    @pl.loop(0, chunks)
    def _(k):
        row_copies(False, k, c_hbm, cv, c_sem)
        chunk_f(k).wait()
        for j in range(CHUNK):
            x = k * CHUNK + j
            cv[x] = cv[x] + step * fv[x, 0:species, :]
        for j in range(CHUNK):
            x = k * CHUNK + j

            @pl.when(flag_ref[0, x] == 0)
            def _():
                row_out(x).start()

    row = lax.broadcasted_iota(jnp.int32, (padded, width), 0)
    extra = lax.broadcasted_iota(jnp.int32, (k_ref.shape[1] // 2 - padded, width), 0)
    ceiling = rate_ceiling * LOG2E

    @pl.loop(0, (count + GROUP - 1) // GROUP)
    def _(g):
        for j in range(GROUP):
            x = place[g * GROUP + j]
            at = slice(j * lanes, (j + 1) * lanes)
            xs[0:species, at] = cv[x]
            xs[species : species + 1, at] = t_ref[pl.ds(x, 1), :]
        x0 = xs[...]
        log1 = jnp.log(jnp.abs(x0) + log_offset)
        inverse = 1.0 / x0[species : species + 1, :]
        full = jnp.concatenate(
            [jnp.where(row == species, 1.0, log1), jnp.where(extra == 0, inverse, 0.0)], axis=0
        )
        hi, lo = split(full)
        terms = jnp.concatenate(
            [jnp.concatenate([hi, hi], axis=0), jnp.concatenate([lo, lo], axis=0)], axis=1
        )
        both = jnp.dot(k_ref[...], terms, preferred_element_type=F32)
        level = both[:, :width] + both[:, width:]
        base[...] = level
        r = jnp.exp2(jnp.minimum(level, ceiling))
        rate[...] = r
        hi, lo = split(r)
        wide = jnp.dot(m_ref[...], hi, preferred_element_type=F32)
        first = wide[:padded] + wide[padded:] + jnp.dot(m_ref[0:padded, :], lo, preferred_element_type=F32)

        def later(state):
            change = jnp.where(row == species, 0.0, jnp.log(jnp.abs(state) + log_offset) - log1)
            change = jnp.concatenate([change, jnp.zeros(extra.shape, F32)], axis=0).astype(BF16)
            level = base[...] + jnp.dot(
                k_ref[:, 0 : k_ref.shape[1] // 2], change, preferred_element_type=F32
            )
            r = jnp.exp2(jnp.minimum(level, ceiling))
            return first + jnp.dot(
                m_ref[0:padded, :], (r - rate[...]).astype(BF16), preferred_element_type=F32
            )

        second = later(x0 + (0.5 * chem_step) * first)
        total = first + 2.0 * second
        third = later(x0 + (0.5 * chem_step) * second)
        total = total + 2.0 * third
        total = total + later(x0 + chem_step * third)
        xs[...] = x0 + (chem_step / 6.0) * total
        for j in range(GROUP):
            x = place[g * GROUP + j]
            at = slice(j * lanes, (j + 1) * lanes)

            @pl.when(g * GROUP + j < count)
            def _():
                cv[x] = xs[0:species, at]
                to_ref[pl.ds(x, 1), :] = xs[species : species + 1, at]
                row_out(x).start()

    @pl.loop(0, rows)
    def _(x):
        row_out(x).wait()


def per_device(
    flow_n, chem_n,
    component_levels, thermal_field, reciprocal_pair_diffusivity, log_arrhenius_factor,
    kinetic_exponents, arrhenius_energies, molar_change_matrix, cooling_by_component, burning_flags,
):
    rows, species, lanes = component_levels.shape
    reactions = kinetic_exponents.shape[0]
    padded = (species + 16) // 16 * 16
    depth = (padded + 1 + 127) // 128 * 128
    chunks = rows // CHUNK

    levels = component_levels.transpose(1, 0, 2)
    vmem = pl.BlockSpec(memory_space=pltpu.VMEM)
    smem = pl.BlockSpec(memory_space=pltpu.SMEM)
    anywhere = pl.BlockSpec(memory_space=pl.ANY)
    flux, step = pl.pallas_call(
        partial(flux_kernel, flow_n, chem_n),
        out_shape=(
            jax.ShapeDtypeStruct((rows, padded, lanes), F32),
            jax.ShapeDtypeStruct((8, lanes), F32),
        ),
        in_specs=[anywhere, vmem, vmem],
        out_specs=(anywhere, vmem),
        scratch_shapes=[
            pltpu.VMEM((rows, species, lanes), F32),
            pltpu.VMEM((rows + 2, padded, lanes), F32),
            pltpu.VMEM((rows + 2, padded, lanes), F32),
            pltpu.VMEM((rows, padded, lanes), F32),
            pltpu.VMEM((padded, depth), F32),
            pltpu.VMEM((2 * padded, 2 * depth), BF16),
            pltpu.VMEM((2, padded, lanes), F32),
            pltpu.VMEM((2, padded, lanes), F32),
            pltpu.VMEM((flow_n + chem_n, 8, lanes), F32),
            pltpu.SemaphoreType.DMA((rows,)),
            pltpu.SemaphoreType.DMA((chunks,)),
            pltpu.SemaphoreType.DMA((4,)),
            pltpu.SemaphoreType.DMA((4,)),
            pltpu.SemaphoreType.DMA((flow_n + chem_n,)),
            pltpu.SemaphoreType.DMA((flow_n + chem_n,)),
        ],
        compiler_params=pltpu.CompilerParams(
            collective_id=0, has_side_effects=True, vmem_limit_bytes=VMEM_BYTES
        ),
        name="flux",
    )(levels, thermal_field, reciprocal_pair_diffusivity)

    advanced, heat = pl.pallas_call(
        burn_kernel,
        out_shape=(
            jax.ShapeDtypeStruct((species, rows, lanes), F32),
            jax.ShapeDtypeStruct((rows, lanes), F32),
        ),
        in_specs=[smem, anywhere, anywhere] + [vmem] * 7,
        out_specs=(anywhere, vmem),
        scratch_shapes=[
            pltpu.VMEM((rows, species, lanes), F32),
            pltpu.VMEM((rows, padded, lanes), F32),
            pltpu.VMEM((padded, GROUP * lanes), F32),
            pltpu.VMEM((reactions, GROUP * lanes), F32),
            pltpu.VMEM((reactions, GROUP * lanes), F32),
            pltpu.VMEM((reactions, depth), F32),
            pltpu.VMEM((depth, (reactions + 127) // 128 * 128), F32),
            pltpu.VMEM((padded, reactions), F32),
            pltpu.VMEM((reactions, 2 * depth), BF16),
            pltpu.VMEM((2 * padded, reactions), BF16),
            pltpu.SMEM((rows + GROUP,), jnp.int32),
            pltpu.SemaphoreType.DMA((rows,)),
            pltpu.SemaphoreType.DMA((chunks,)),
            pltpu.SemaphoreType.DMA(()),
        ],
        compiler_params=pltpu.CompilerParams(vmem_limit_bytes=VMEM_BYTES),
        name="burn",
    )(
        burning_flags.T, levels, flux, thermal_field, step, log_arrhenius_factor,
        kinetic_exponents, arrhenius_energies, molar_change_matrix, cooling_by_component[None],
    )
    return advanced.transpose(1, 0, 2), heat


def solution(mesh):
    placed = (
        P("flow", None, "chem"),
        P("flow", "chem"),
        P(),
        P(),
        P(),
        P(),
        P(),
        P(),
        P("flow", "chem"),
    )
    return jax.shard_map(
        partial(per_device, mesh.shape["flow"], mesh.shape["chem"]),
        mesh=mesh,
        in_specs=placed,
        out_specs=(P("flow", None, "chem"), P("flow", "chem")),
        check_vma=False,
    )
```

```python
from functools import partial
import math

import jax
import jax.numpy as jnp
from jax import lax
from jax.experimental import pallas as pl
from jax.experimental.pallas import tpu as pltpu
from jax.sharding import PartitionSpec as P

MESH = pl.DeviceIdType.MESH
F32 = jnp.float32
BF16 = jnp.bfloat16
courant = 0.2
chem_step = 0.05
log_offset = 0.001
rate_ceiling = 2.0
LOG2E = 1.0 / math.log(2.0)
CHUNK = 8
GROUP = 8
WIDE = 8
VMEM_BYTES = 56 * 2**20


def split(x):
    hi = x.astype(BF16)
    return hi, (x - hi.astype(F32)).astype(BF16)


def row_copies(start, k, species_hbm, rows_vmem, sem):
    for j in range(CHUNK):
        x = k * CHUNK + j
        copy = pltpu.make_async_copy(species_hbm.at[:, x], rows_vmem.at[x], sem.at[x])
        if start:
            copy.start()
        else:
            copy.wait()


def flux_kernel(
    flow_n, chem_n, c_hbm, t_ref, pair_ref, f_hbm, dt_ref,
    cv, cx, dx, fv, pairs, rr_ref, col_out, col_in, peak,
    in_sem, out_sem, halo_send, halo_recv, max_send, max_recv,
):
    rows, species, lanes = cv.shape
    padded = cx.shape[1]
    depth = pairs.shape[1]
    chunks = rows // CHUNK
    fi, ci = lax.axis_index("flow"), lax.axis_index("chem")

    def chunk_out(k):
        at = pl.ds(k * CHUNK, CHUNK)
        return pltpu.make_async_copy(fv.at[at], f_hbm.at[at], out_sem.at[k])

    @pl.loop(0, chunks)
    def _(k):
        row_copies(True, k, c_hbm, cv, in_sem)

    barrier = pltpu.get_barrier_semaphore()
    for k in range(1, flow_n):
        pl.semaphore_signal(barrier, inc=1, device_id=(lax.rem(fi + k, flow_n), ci), device_id_type=MESH)
    for k in range(1, chem_n):
        pl.semaphore_signal(barrier, inc=1, device_id=(fi, lax.rem(ci + k, chem_n)), device_id_type=MESH)

    at_col = lax.broadcasted_iota(jnp.int32, pairs.shape, 1)
    pairs[...] = jnp.where(at_col < species, 1.0, 0.0)
    pairs[0:species, 0:species] = pair_ref[...]
    hi, lo = split(pairs[...])
    rr_ref[...] = jnp.concatenate(
        [jnp.concatenate([hi, hi], axis=1), jnp.concatenate([lo, lo], axis=1)], axis=0
    )

    lane = lax.broadcasted_iota(jnp.int32, (padded, lanes), 1)

    def prepare(k, cols):
        row_copies(False, k, c_hbm, cv, in_sem)
        cx[pl.ds(k * CHUNK + 1, CHUNK), 0:species, :] = cv[pl.ds(k * CHUNK, CHUNK)]
        for j in range(CHUNK):
            x = k * CHUNK + j
            cx[x + 1, species : species + 1, :] = t_ref[pl.ds(x, 1), :]
        cols = pltpu.roll(cols, lanes - 2 * CHUNK, 1)
        for j in range(CHUNK):
            at = lanes - 2 * CHUNK + 2 * j
            edges = pltpu.roll(cx[k * CHUNK + j + 1], at + 1, 1)
            cols = jnp.where((lane == at) | (lane == at + 1), edges, cols)
        return cols

    cols = lax.fori_loop(0, chunks, prepare, jnp.ones((padded, lanes), F32))
    cols = pltpu.roll(cols, 2 * rows, 1) if 2 * rows < lanes else cols
    col_out[0] = pltpu.roll(cols, lanes - 2, 1)
    col_out[1] = cols
    pl.semaphore_wait(barrier, flow_n + chem_n - 2)

    before, after = lax.rem(fi + flow_n - 1, flow_n), lax.rem(fi + 1, flow_n)
    west, east = lax.rem(ci + chem_n - 1, chem_n), lax.rem(ci + 1, chem_n)

    def halo(k, src, dst, device):
        return pltpu.make_async_remote_copy(
            src_ref=src, dst_ref=dst, send_sem=halo_send.at[k], recv_sem=halo_recv.at[k],
            device_id=device, device_id_type=MESH,
        )

    halos = [
        halo(0, cx.at[1], cx.at[rows + 1], (before, ci)),
        halo(1, cx.at[rows], cx.at[0], (after, ci)),
        halo(2, col_out.at[0], col_in.at[1], (fi, west)),
        halo(3, col_out.at[1], col_in.at[0], (fi, east)),
    ]
    for copy in halos:
        copy.start()

    def spreading(block):
        hi, lo = split(block)
        blank = jnp.zeros((depth - padded, block.shape[1]), BF16)
        total = jnp.dot(
            rr_ref[...], jnp.concatenate([hi, blank, lo, blank], axis=0), preferred_element_type=F32
        )
        heat = block[species : species + 1, :]
        total = total[:padded] + total[padded:]
        guess = pl.reciprocal(total, approx=True)
        guess = guess * (2.0 - total * guess)
        return heat * jnp.sqrt(heat) * (guess * (2.0 - total * guess))

    def diffusivities(k, top):
        first = k * CHUNK + 1
        d = spreading(jnp.concatenate([cx[first + j] for j in range(CHUNK)], axis=1))
        m = d[:, :lanes]
        for j in range(CHUNK):
            here = d[:, j * lanes : (j + 1) * lanes]
            dx[first + j] = here
            m = jnp.maximum(m, here)
        for s in range(0, padded, 8):
            top = jnp.maximum(top, m[s : s + 8])
        return top

    peak[0] = lax.fori_loop(0, chunks, diffusivities, jnp.zeros((8, lanes), F32))

    def spread_max(base, count, who):
        return [
            pltpu.make_async_remote_copy(
                src_ref=peak.at[base], dst_ref=peak.at[base + k],
                send_sem=max_send.at[base + k], recv_sem=max_recv.at[base + k],
                device_id=who(k), device_id_type=MESH,
            )
            for k in range(1, count)
        ]

    first = spread_max(0, flow_n, lambda k: (lax.rem(fi + k, flow_n), ci))
    for copy in first:
        copy.start()

    for copy in halos:
        copy.wait()
    zero = jnp.zeros((padded, lanes), F32)
    side = jnp.where(lax.rem(lane, 2) == 0, col_in[0], col_in[1])
    own = pltpu.roll(col_out[1], lanes - 1, 1)
    d = spreading(jnp.concatenate([cx[0], cx[rows + 1], side, own], axis=1))
    dx[0] = jnp.where(fi == 0, zero, d[:, :lanes])
    dx[rows + 1] = jnp.where(fi == flow_n - 1, zero, d[:, lanes : 2 * lanes])
    cx[0] = jnp.where(fi == 0, zero, cx[0])
    cx[rows + 1] = jnp.where(fi == flow_n - 1, zero, cx[rows + 1])
    outside = (lax.rem(lane, 2) == 0) & (ci == 0) | (lax.rem(lane, 2) == 1) & (ci == chem_n - 1)
    side_c = jnp.where(outside, zero, side)
    side_d = jnp.where(outside, zero, d[:, 2 * lanes : 3 * lanes])
    edge = (side_d + d[:, 3 * lanes :]) * (own - side_c)
    col_in[0] = jnp.where(lax.rem(lane, 2) == 0, edge, -edge)

    wide = (WIDE, padded, lanes)
    at_lane = lax.broadcasted_iota(jnp.int32, wide, 2)

    def flux_chunk(k):
        edges = col_in[0]
        for j in range(0, CHUNK, WIDE):
            x = k * CHUNK + j
            c, d = cx[pl.ds(x, WIDE + 2)], dx[pl.ds(x, WIDE + 2)]
            c0, d0 = c[1:-1], d[1:-1]
            edge = jnp.stack(
                [
                    pltpu.roll(edges, lanes - 2 * (j + i), 1) if j + i else edges
                    for i in range(WIDE)
                ]
            )
            left = (pltpu.roll(d0, 1, 2) + d0) * (c0 - pltpu.roll(c0, 1, 2))
            left = jnp.where(at_lane == 0, edge, left)
            right = jnp.where(at_lane == lanes - 1, edge, pltpu.roll(left, lanes - 1, 2))
            face = (d[1:] + d[:-1]) * (c[1:] - c[:-1])
            fv[pl.ds(x, WIDE)] = 0.5 * ((face[1:] - face[:-1]) + (right - left))
        col_in[0] = pltpu.roll(edges, lanes - 2 * CHUNK, 1)
        chunk_out(k).start()

    pl.loop(0, chunks // 2)(flux_chunk)

    for copy in first:
        copy.wait()
    top = peak[0]
    for k in range(1, flow_n):
        top = jnp.maximum(top, peak[k])
    peak[flow_n] = top
    second = spread_max(flow_n, chem_n, lambda k: (fi, lax.rem(ci + k, chem_n)))
    for copy in second:
        copy.start()
    pl.loop(chunks // 2, chunks)(flux_chunk)
    for copy in second:
        copy.wait()
    for k in range(1, chem_n):
        top = jnp.maximum(top, peak[flow_n + k])
    dt_ref[...] = courant / jnp.broadcast_to(
        jnp.max(jnp.max(top, axis=1, keepdims=True), axis=0, keepdims=True), dt_ref.shape
    )

    @pl.loop(0, chunks)
    def _(k):
        chunk_out(k).wait()


def burn_kernel(
    flag_ref, c_hbm, f_hbm, t_ref, dt_ref, factor_ref, order_ref, energy_ref, change_ref, cool_ref,
    o_hbm, to_ref,
    cv, fv, xs, base, rate, wide_k, side_k, wide_m, k_ref, m_ref, place, c_sem, f_sem, o_sem,
):
    rows, species, lanes = cv.shape
    padded = fv.shape[1]
    depth = wide_k.shape[1]
    reactions = wide_k.shape[0]
    chunks = rows // CHUNK
    width = GROUP * lanes

    def chunk_f(k):
        at = pl.ds(k * CHUNK, CHUNK)
        return pltpu.make_async_copy(f_hbm.at[at], fv.at[at], f_sem.at[k])

    def row_out(x):
        return pltpu.make_async_copy(cv.at[x], o_hbm.at[:, x], o_sem)

    @pl.loop(0, chunks)
    def _(k):
        row_copies(True, k, c_hbm, cv, c_sem)
        chunk_f(k).start()

    to_ref[...] = t_ref[...]

    def listed(x, count):
        place[count] = x
        return count + flag_ref[0, x]

    count = lax.fori_loop(0, rows, listed, jnp.int32(0), unroll=8)
    last = place[jnp.maximum(count - 1, 0)]
    for j in range(GROUP):
        place[count + j] = last

    wide_k[...] = jnp.zeros(wide_k.shape, F32)
    wide_k[:, 0:species] = order_ref[...]
    side_k[...] = jnp.zeros(side_k.shape, F32)
    side_k[species : species + 1, 0:reactions] = factor_ref[...].reshape(1, reactions)
    side_k[padded : padded + 1, 0:reactions] = -energy_ref[...].reshape(1, reactions)
    hi, lo = split((wide_k[...] + side_k[...].T[0:reactions, :]) * LOG2E)
    k_ref[:, 0:depth] = hi
    k_ref[:, depth:] = lo
    cooled = jnp.dot(
        jnp.broadcast_to(cool_ref[...], (8, species)), change_ref[...],
        precision=lax.Precision.HIGHEST, preferred_element_type=F32,
    )
    wide_m[...] = jnp.zeros(wide_m.shape, F32)
    wide_m[0:species, :] = change_ref[...]
    wide_m[species : species + 1, :] = -cooled[0:1]
    hi, lo = split(wide_m[...])
    m_ref[0:padded, :] = hi
    m_ref[padded:, :] = lo

    step = dt_ref[0:1, :]

    @pl.loop(0, chunks)
    def _(k):
        row_copies(False, k, c_hbm, cv, c_sem)
        chunk_f(k).wait()
        here = pl.ds(k * CHUNK, CHUNK)
        cv[here] = cv[here] + step * fv[here, 0:species, :]
        for j in range(CHUNK):
            x = k * CHUNK + j

            @pl.when(flag_ref[0, x] == 0)
            def _():
                row_out(x).start()

    row = lax.broadcasted_iota(jnp.int32, (padded, width), 0)
    extra = lax.broadcasted_iota(jnp.int32, (k_ref.shape[1] // 2 - padded, width), 0)
    ceiling = rate_ceiling * LOG2E

    @pl.loop(0, (count + GROUP - 1) // GROUP)
    def _(g):
        for j in range(GROUP):
            x = place[g * GROUP + j]
            at = slice(j * lanes, (j + 1) * lanes)
            xs[0:species, at] = cv[x]
            xs[species : species + 1, at] = t_ref[pl.ds(x, 1), :]
        x0 = xs[...]
        log1 = jnp.log(jnp.abs(x0) + log_offset)
        inverse = 1.0 / x0[species : species + 1, :]
        full = jnp.concatenate(
            [jnp.where(row == species, 1.0, log1), jnp.where(extra == 0, inverse, 0.0)], axis=0
        )
        hi, lo = split(full)
        terms = jnp.concatenate(
            [jnp.concatenate([hi, hi], axis=0), jnp.concatenate([lo, lo], axis=0)], axis=1
        )
        both = jnp.dot(k_ref[...], terms, preferred_element_type=F32)
        level = both[:, :width] + both[:, width:]
        base[...] = level
        r = jnp.exp2(jnp.minimum(level, ceiling))
        rate[...] = r
        hi, lo = split(r)
        wide = jnp.dot(m_ref[...], hi, preferred_element_type=F32)
        first = wide[:padded] + wide[padded:] + jnp.dot(m_ref[0:padded, :], lo, preferred_element_type=F32)

        def later(state):
            change = jnp.where(row == species, 0.0, jnp.log(jnp.abs(state) + log_offset) - log1)
            change = jnp.concatenate([change, jnp.zeros(extra.shape, F32)], axis=0).astype(BF16)
            level = base[...] + jnp.dot(
                k_ref[:, 0 : k_ref.shape[1] // 2], change, preferred_element_type=F32
            )
            r = jnp.exp2(jnp.minimum(level, ceiling))
            return first + jnp.dot(
                m_ref[0:padded, :], (r - rate[...]).astype(BF16), preferred_element_type=F32
            )

        second = later(x0 + (0.5 * chem_step) * first)
        total = first + 2.0 * second
        third = later(x0 + (0.5 * chem_step) * second)
        total = total + 2.0 * third
        total = total + later(x0 + chem_step * third)
        xs[...] = x0 + (chem_step / 6.0) * total
        for j in range(GROUP):
            x = place[g * GROUP + j]
            at = slice(j * lanes, (j + 1) * lanes)

            @pl.when(g * GROUP + j < count)
            def _():
                cv[x] = xs[0:species, at]
                to_ref[pl.ds(x, 1), :] = xs[species : species + 1, at]
                row_out(x).start()

    @pl.loop(0, rows)
    def _(x):
        row_out(x).wait()


def per_device(
    flow_n, chem_n,
    component_levels, thermal_field, reciprocal_pair_diffusivity, log_arrhenius_factor,
    kinetic_exponents, arrhenius_energies, molar_change_matrix, cooling_by_component, burning_flags,
):
    rows, species, lanes = component_levels.shape
    reactions = kinetic_exponents.shape[0]
    padded = (species + 16) // 16 * 16
    depth = (padded + 1 + 127) // 128 * 128
    chunks = rows // CHUNK

    levels = component_levels.transpose(1, 0, 2)
    vmem = pl.BlockSpec(memory_space=pltpu.VMEM)
    smem = pl.BlockSpec(memory_space=pltpu.SMEM)
    anywhere = pl.BlockSpec(memory_space=pl.ANY)
    flux, step = pl.pallas_call(
        partial(flux_kernel, flow_n, chem_n),
        out_shape=(
            jax.ShapeDtypeStruct((rows, padded, lanes), F32),
            jax.ShapeDtypeStruct((8, lanes), F32),
        ),
        in_specs=[anywhere, vmem, vmem],
        out_specs=(anywhere, vmem),
        scratch_shapes=[
            pltpu.VMEM((rows, species, lanes), F32),
            pltpu.VMEM((rows + 2, padded, lanes), F32),
            pltpu.VMEM((rows + 2, padded, lanes), F32),
            pltpu.VMEM((rows, padded, lanes), F32),
            pltpu.VMEM((padded, depth), F32),
            pltpu.VMEM((2 * padded, 2 * depth), BF16),
            pltpu.VMEM((2, padded, lanes), F32),
            pltpu.VMEM((2, padded, lanes), F32),
            pltpu.VMEM((flow_n + chem_n, 8, lanes), F32),
            pltpu.SemaphoreType.DMA((rows,)),
            pltpu.SemaphoreType.DMA((chunks,)),
            pltpu.SemaphoreType.DMA((4,)),
            pltpu.SemaphoreType.DMA((4,)),
            pltpu.SemaphoreType.DMA((flow_n + chem_n,)),
            pltpu.SemaphoreType.DMA((flow_n + chem_n,)),
        ],
        compiler_params=pltpu.CompilerParams(
            collective_id=0, has_side_effects=True, vmem_limit_bytes=VMEM_BYTES
        ),
        name="flux",
    )(levels, thermal_field, reciprocal_pair_diffusivity)

    advanced, heat = pl.pallas_call(
        burn_kernel,
        out_shape=(
            jax.ShapeDtypeStruct((species, rows, lanes), F32),
            jax.ShapeDtypeStruct((rows, lanes), F32),
        ),
        in_specs=[smem, anywhere, anywhere] + [vmem] * 7,
        out_specs=(anywhere, vmem),
        scratch_shapes=[
            pltpu.VMEM((rows, species, lanes), F32),
            pltpu.VMEM((rows, padded, lanes), F32),
            pltpu.VMEM((padded, GROUP * lanes), F32),
            pltpu.VMEM((reactions, GROUP * lanes), F32),
            pltpu.VMEM((reactions, GROUP * lanes), F32),
            pltpu.VMEM((reactions, depth), F32),
            pltpu.VMEM((depth, (reactions + 127) // 128 * 128), F32),
            pltpu.VMEM((padded, reactions), F32),
            pltpu.VMEM((reactions, 2 * depth), BF16),
            pltpu.VMEM((2 * padded, reactions), BF16),
            pltpu.SMEM((rows + GROUP,), jnp.int32),
            pltpu.SemaphoreType.DMA((rows,)),
            pltpu.SemaphoreType.DMA((chunks,)),
            pltpu.SemaphoreType.DMA(()),
        ],
        compiler_params=pltpu.CompilerParams(vmem_limit_bytes=VMEM_BYTES),
        name="burn",
    )(
        burning_flags.T, levels, flux, thermal_field, step, log_arrhenius_factor,
        kinetic_exponents, arrhenius_energies, molar_change_matrix, cooling_by_component[None],
    )
    return advanced.transpose(1, 0, 2), heat


def solution(mesh):
    placed = (
        P("flow", None, "chem"),
        P("flow", "chem"),
        P(),
        P(),
        P(),
        P(),
        P(),
        P(),
        P("flow", "chem"),
    )
    return jax.shard_map(
        partial(per_device, mesh.shape["flow"], mesh.shape["chem"]),
        mesh=mesh,
        in_specs=placed,
        out_specs=(P("flow", None, "chem"), P("flow", "chem")),
        check_vma=False,
    )
```
